32 devices in a mesh: metro: 2 (over y), region: 8 (over z, x), dest: 2 (over core).
Axes of the slice: x: 2, y: 2, z: 4, core: 2. Of those that a mesh axis runs over, the one named last changes fastest.
Arguments:
- transitions: bfloat16 [256, 6, 128, 128], P(('metro', 'region')), parts along dimension 0, may hold values from 0 to 0.6
- tile_cols: int32 [256, 6], P(('metro', 'region')), parts along dimension 0, may hold values from 0 to 19, as said below
- tile_count: int32 [256], P(('metro', 'region')), parts along dimension 0, may hold values from 1 to 6
- publish: int32 [16, 4, 128], P(('metro', 'region')), parts along dimension 0, may hold values from 0 to 2047
- reward: float32 [32768], P(('metro', 'region')), parts along dimension 0, may hold values from -1 to 0
- value_init: bfloat16 [32768, 256], P(('metro', 'region'), 'dest'), parts along dimension 0, may hold values from -3 to 3
- anchor: bfloat16 [32768, 256], P(('metro', 'region'), 'dest'), parts along dimension 0, may hold values from 0.0009994507 to 0.0099487305
- goal_segment_index: int32 [512], P(('metro', 'dest')), parts along dimension 0, may hold values from 0 to 16383
- routes: int32 [512, 64], P(('metro', 'dest')), parts along dimension 0, may hold values from 0 to 16383
Outputs:
- reward_grad: float32 [32768], P(('metro', 'region', 'dest')), parts along dimension 0
The draws below stay inside these ranges and needn't reach their ends.
There are 2 independent parts, one for each index of `metro`. The reference program is written for one: setup_inputs(seed, part) draws one part's arguments, and reference() takes and returns one part's arrays. A program takes and returns all parts, laid end to end along the dimension named above; each array names one. Nothing has to cross between parts.
Inputs may be any that keep to these rules, and one draw needn't show every extreme that they name: `tile_cols`: tile 0 of every block row names one of the region's own blocks (a value under 16); values 16 + j name the boundary block of offset j; tiles at k >= tile_count of their block row are padding with arbitrary contents.
All inputs are finite; a program needn't handle non-finite values.
Results may differ from the reference program's by a relative error of at most 0.0003.
Values may be sent and summed in bfloat16 or wider, within the bound.
A program may use at most 64 MiB of HBM per device.

```python
import math
import jax
import jax.numpy as jnp
from jax import lax

TILE = 128
BLK_DEV = 16
KMAX = 6
GOAL_COUNT = 256
ROUTE_LEN = 64
SEG_DEV = 2048
ROAD_PIECES = 16384
BLOCKS = 128
REGIONS = 8
N_REGION = 8


def row_weights(key, shape_rows, low, high):
    return jnp.exp(jax.random.uniform(key, shape_rows, jnp.float32, math.log(low), math.log(high)))


def draw_transitions(key, part):
    key = jax.random.fold_in(key, 11)
    keys = jax.random.split(key, 6)
    full_shape = (BLOCKS, KMAX, TILE, TILE)
    shape_rows = (BLOCKS, KMAX, TILE, 1)
    offset_tile = jax.random.randint(keys[0], (BLOCKS, KMAX, 1, 1), 0, TILE)
    extra_col = jax.random.randint(keys[1], shape_rows, 0, TILE)
    row_pos = lax.broadcasted_iota(jnp.int32, full_shape, 2)
    col_pos = lax.broadcasted_iota(jnp.int32, full_shape, 3)
    main_col = (row_pos + offset_tile) % TILE
    main_w = row_weights(keys[2], shape_rows, 0.06, 0.25)
    extra_w = row_weights(keys[3], shape_rows, 0.02, 0.12)
    background = row_weights(keys[5], full_shape, 0.0008, 0.004)
    main_part = jnp.where(col_pos == main_col, main_w, 0.0)
    extra_part = jnp.where(col_pos == extra_col, extra_w, 0.0)
    whole = main_part + extra_part + background
    return jnp.minimum(whole, 0.6).astype(jnp.bfloat16)


def draw_tile_cols(key, part):
    key = jax.random.fold_in(key, 23)
    first_key, rest_key = jax.random.split(key)
    first_cols = jax.random.randint(first_key, (BLOCKS, 1), 0, BLK_DEV)
    rest_cols = jax.random.randint(rest_key, (BLOCKS, KMAX - 1), 0, BLK_DEV + 4)
    return jnp.concatenate([first_cols, rest_cols], 1).astype(jnp.int32)


def plant(values, own_key, smallest, top_value):
    longest = values.shape.index(max(values.shape))
    spots = []
    for shift in (0, 1):
        where = [jax.random.randint(jax.random.fold_in(own_key, axis), (), 0, length) for axis, length in enumerate(values.shape)]
        where[longest] = (where[longest] + shift) % values.shape[longest]
        spots.append(tuple(where))
    return values.at[spots[0]].set(smallest).at[spots[1]].set(top_value)


def level_of(rng, extent, cuts, least, largest):
    factor_of = 1.0
    for position, parts in cuts:
        heights = jax.random.uniform(jax.random.fold_in(jax.random.fold_in(rng, 6), position), (parts,), jnp.float32, least / len(cuts), largest / len(cuts))
        factor_of = factor_of * jnp.repeat(jnp.exp(heights), extent[position] // parts).reshape((-1,) + (1,) * (len(extent) - 1 - position))
    return factor_of


def normal_values(own_key, dims, spread, bound, cuts=(), held_as=jnp.bfloat16):
    values = spread * jax.random.normal(own_key, dims, jnp.float32)
    if cuts:
        values = values * level_of(own_key, dims, cuts, -0.22, 0.18)
    return jnp.clip(values, -bound, bound).astype(held_as)


def setup_inputs(seed: int = 0, part: int = 0) -> dict:
    streams_of = jax.random.split(jax.random.key(seed), 10)
    part_keys = jax.random.split(jax.random.fold_in(streams_of[9], part), 10)
    transitions = draw_transitions(jax.random.fold_in(jax.random.fold_in(streams_of[9], part), 71), part)
    tile_cols = draw_tile_cols(jax.random.fold_in(jax.random.fold_in(streams_of[9], part), 71), part)
    tile_count = plant(jax.random.randint(part_keys[2], (BLOCKS,), 1, KMAX + 1), jax.random.fold_in(part_keys[2], 1), 1, KMAX).astype(jnp.int32)
    publish = plant(jax.random.randint(part_keys[3], (REGIONS, 4, TILE), 0, SEG_DEV), jax.random.fold_in(part_keys[3], 1), 0, SEG_DEV - 1).astype(jnp.int32)
    reward = jnp.clip(-1.0 + 1.0 * jax.random.uniform(part_keys[4], (ROAD_PIECES,), jnp.float32) ** level_of(part_keys[4], (ROAD_PIECES,), ((0, 8),), -0.2, 0.2), -1.0, 0.0)
    value_init = normal_values(part_keys[5], (ROAD_PIECES, GOAL_COUNT), 0.5, 3.0, ((0, 8), (1, 2)))
    anchor = jnp.clip(jnp.exp(math.log(0.0099487305) - 2.2979944 * jax.random.uniform(part_keys[6], (ROAD_PIECES, GOAL_COUNT), jnp.float32) ** level_of(part_keys[6], (ROAD_PIECES, GOAL_COUNT), ((0, 8), (1, 2)), -0.2, 0.2)), 0.0009994507, 0.0099487305).astype(jnp.bfloat16)
    goal_segment_index = plant(jax.random.randint(part_keys[7], (GOAL_COUNT,), 0, ROAD_PIECES), jax.random.fold_in(part_keys[7], 1), 0, ROAD_PIECES - 1).astype(jnp.int32)
    routes = plant(jax.random.randint(part_keys[8], (GOAL_COUNT, ROUTE_LEN), 0, ROAD_PIECES), jax.random.fold_in(part_keys[8], 1), 0, ROAD_PIECES - 1).astype(jnp.int32)
    return {"transitions": transitions, "tile_cols": tile_cols, "tile_count": tile_count, "publish": publish, "reward": reward, "value_init": value_init, "anchor": anchor, "goal_segment_index": goal_segment_index, "routes": routes}


OFFSETS = (-2, -1, 1, 2)


def region_shift(field, offset):
    padding = jnp.zeros((abs(offset),) + field.shape[1:], field.dtype)
    if offset > 0:
        return jnp.concatenate([field[offset:], padding], 0)
    return jnp.concatenate([padding, field[:offset]], 0)


def take_rows(values, indices):
    return values[indices]


def add_rows(values, indices, extra):
    return values.at[indices].add(extra)


def extend(zfield, publish):
    zregions = zfield.reshape(N_REGION, SEG_DEV, GOAL_COUNT)
    pieces = jax.vmap(take_rows)(zregions, publish)
    boundary = jnp.stack([region_shift(pieces[:, slot_index], offset) for slot_index, offset in enumerate(OFFSETS)], 1)
    own_blocks = zregions.reshape(N_REGION, BLK_DEV, TILE, GOAL_COUNT)
    return jnp.concatenate([own_blocks, boundary], 1)


def reference(transitions, tile_cols, tile_count, publish, reward, value_init, anchor, goal_segment_index, routes):
    live_mask = jnp.arange(KMAX, dtype=jnp.int32)[None, :] < tile_count[:, None]
    tiles_reg = transitions.reshape(N_REGION, BLK_DEV, KMAX, TILE, TILE)
    cols_reg = tile_cols.reshape(N_REGION, BLK_DEV, KMAX)
    mask_reg = live_mask.reshape(N_REGION, BLK_DEV, KMAX)
    segment_index = jnp.arange(ROAD_PIECES, dtype=jnp.int32)
    leaving_reward = (segment_index[:, None] == goal_segment_index[None, :]).astype(jnp.float32)

    def backup_region(operands):
        tile_part, cols_part, mask_part, extended = operands
        picked = extended[cols_part] * mask_part.astype(jnp.bfloat16)[:, :, None, None]
        return jnp.einsum("bkij,bkjd->bid", tile_part.astype(jnp.float32), picked.astype(jnp.float32))

    def backup(zfield):
        extended = extend(zfield, publish)
        total_sum = lax.map(backup_region, (tiles_reg, cols_reg, mask_reg, extended))
        return reward[:, None] + jnp.log(total_sum.reshape(ROAD_PIECES, GOAL_COUNT) + leaving_reward)

    z_start = jnp.exp(value_init.astype(jnp.float32)).astype(jnp.bfloat16)
    value_one = backup(z_start)
    z_one = jnp.exp(value_one).astype(jnp.bfloat16)
    value_two = backup(z_one)
    weight_rows = jnp.exp(reward[:, None] - value_two)
    anchor_flow = anchor.astype(jnp.float32)

    def spread_region(operands):
        tile_part, cols_part, mask_part, weighted = operands
        contrib = jnp.einsum("bkij,bid->bkjd", tile_part.astype(jnp.float32), weighted.astype(jnp.float32))
        contrib = contrib * mask_part.astype(jnp.float32)[:, :, None, None]
        padding = jnp.zeros((BLK_DEV + 4, TILE, GOAL_COUNT), jnp.float32)
        return padding.at[cols_part].add(contrib)

    def sweep(flow):
        weighted = (flow * weight_rows).astype(jnp.bfloat16).reshape(N_REGION, BLK_DEV, TILE, GOAL_COUNT)
        folded = lax.map(spread_region, (tiles_reg, cols_reg, mask_reg, weighted))
        local_flow = folded[:, :BLK_DEV].reshape(N_REGION, SEG_DEV, GOAL_COUNT)
        for slot_index, offset in enumerate(OFFSETS):
            arrived = region_shift(folded[:, BLK_DEV + slot_index], -offset)
            local_flow = jax.vmap(add_rows)(local_flow, publish[:, slot_index], arrived)
        return anchor_flow + z_one.astype(jnp.float32) * local_flow.reshape(ROAD_PIECES, GOAL_COUNT)

    flow_one = sweep(anchor_flow)
    flow_two = sweep(flow_one)
    visits = anchor_flow + flow_one + flow_two
    dest_cols = jnp.arange(GOAL_COUNT, dtype=jnp.int32)[:, None]
    counts = jnp.zeros((ROAD_PIECES, GOAL_COUNT), jnp.float32).at[routes, dest_cols].add(1.0)
    return jnp.sum(counts - visits, axis=1)
```

```python
import functools

import jax
import jax.numpy as jnp
from jax import lax
from jax.experimental import pallas as pl
from jax.experimental.pallas import tpu as pltpu
from jax.sharding import PartitionSpec as P

OFFSETS = (-2, -1, 1, 2)
MESH = pl.DeviceIdType.MESH
F32 = jnp.float32
BF16 = jnp.bfloat16
LAST = (((1,), (1,)), ((), ()))


def dims(blocks, kmax):
    tiles = blocks * kmax
    cols = blocks + 4
    pairs = (tiles + cols) // 2
    return tiles, cols, pairs


def plan(tile_cols, tile_count):
    blocks, kmax = tile_cols.shape
    tiles, cols, pairs = dims(blocks, kmax)
    live = lax.broadcasted_iota(jnp.int32, (blocks, kmax), 1) < tile_count[:, None]
    col = jnp.where(live, tile_cols, cols).reshape(tiles)
    tile = jnp.arange(tiles, dtype=jnp.int32)
    cid = jnp.arange(cols, dtype=jnp.int32)
    same = col[:, None] == col[None, :]
    rank = jnp.sum((same & (tile[None, :] < tile[:, None])).astype(jnp.int32), 1)
    count = jnp.sum((col[:, None] == cid[None, :]).astype(jnp.int32), 0)
    padded = (count + 1) // 2 * 2
    start = jnp.sum(jnp.where(cid[None, :] < cid[:, None], padded[None, :], 0), 1)
    first = jnp.sum(jnp.where(cid[None, :] < col[:, None], padded[None, :], 0), 1)
    spot = jnp.where(col < cols, first + rank, -1)
    slot = jnp.arange(2 * pairs, dtype=jnp.int32)
    hit = slot[:, None] == spot[None, :]
    tile_at = jnp.sum(jnp.where(hit, tile[None, :], 0), 1)
    block_at = blocks + jnp.sum(jnp.where(hit, (tile // kmax - blocks)[None, :], 0), 1)
    pair = jnp.arange(pairs, dtype=jnp.int32)
    fresh = jnp.any((pair[:, None] * 2 == start[None, :]) & (count[None, :] > 0), 1)
    keep = 1 - fresh.astype(jnp.int32)
    last = jnp.where(count > 0, (start + padded) // 2 - 1, pairs)
    return jnp.concatenate([col, tile_at, block_at, keep, last])


def kernel(
    shape,
    lists,
    publish,
    reward,
    goal,
    routes,
    trans_hbm,
    init_hbm,
    anchor_hbm,
    out,
    trans,
    init,
    anchor_in,
    anchor,
    ext1,
    ext2,
    piece1,
    piece2,
    hot,
    ids,
    gap,
    inv,
    flow_u,
    sums,
    part1,
    part2,
    arr1,
    arr2,
    total,
    other,
    load_sem,
    send_sem,
    recv_sem,
    dest_sem,
):
    blocks, kmax, regions = shape
    tiles, cols, pairs = dims(blocks, kmax)
    tile = 128
    me = lax.axis_index("region")
    side = lax.axis_index("dest")
    first_seg = me * (blocks * tile)
    at_tile, at_block = tiles, tiles + 2 * pairs
    at_keep = tiles + 4 * pairs
    at_last = at_keep + pairs

    load_init = pltpu.make_async_copy(init_hbm, init, load_sem.at[0])
    load_trans = pltpu.make_async_copy(trans_hbm, trans, load_sem.at[1])
    load_anchor = pltpu.make_async_copy(anchor_hbm, anchor_in, load_sem.at[2])
    load_init.start()
    load_trans.start()
    load_anchor.start()

    def inside(by):
        return (me + by >= 0) & (me + by < regions)

    barrier = pltpu.get_barrier_semaphore()
    pl.semaphore_signal(barrier, inc=1, device_id={"dest": 1 - side}, device_id_type=MESH)
    for by in OFFSETS:
        @pl.when(inside(by))
        def _():
            pl.semaphore_signal(barrier, inc=1, device_id={"region": me + by}, device_id_type=MESH)

    zero = jnp.zeros((tile, tile), BF16)
    ext1[cols] = zero
    ext2[cols] = zero
    flow_u[blocks] = zero
    sums[pairs] = jnp.zeros((tile, tile), F32)
    for j, by in enumerate(OFFSETS):
        @pl.when(jnp.logical_not(inside(by)))
        def _():
            ext1[blocks + j] = zero
            ext2[blocks + j] = zero

        @pl.when(jnp.logical_not(inside(-by)))
        def _():
            arr1[j] = zero
            arr2[j] = zero

    row = lax.broadcasted_iota(jnp.int32, (tile, tile), 0)
    lane = lax.broadcasted_iota(jnp.int32, (tile, tile), 1)

    def make_hot(c, carry):
        for j in range(4):
            pub = publish[j : j + 1, :]
            hit = (row + c * tile) == pub
            hot[j, pl.ds(pl.multiple_of(c * tile, tile), tile), :] = jnp.where(hit, 1.0, 0.0).astype(BF16)
        return carry

    lax.fori_loop(0, blocks, make_hot, 0)

    load_init.wait()

    def make_start(b, carry):
        block = init[pl.ds(pl.multiple_of(b * tile, tile), tile), :].astype(F32)
        ext1[b] = jnp.exp(block.T).astype(BF16)
        return carry

    lax.fori_loop(0, blocks, make_start, 0, unroll=2)

    def exchange(phase, source, target, base, sign):
        def copy(j):
            return pltpu.make_async_remote_copy(
                src_ref=source.at[j],
                dst_ref=target.at[base + j],
                send_sem=send_sem.at[phase, j],
                recv_sem=recv_sem.at[phase, j],
                device_id={"region": me + sign * OFFSETS[j]},
                device_id_type=MESH,
            )

        def start(j):
            @pl.when(inside(sign * OFFSETS[j]))
            def _():
                copy(j).start()

        def wait():
            for j in range(4):
                @pl.when(inside(-sign * OFFSETS[j]))
                def _():
                    copy(j).wait_recv()

        def finish():
            for j in range(4):
                @pl.when(inside(sign * OFFSETS[j]))
                def _():
                    copy(j).wait_send()

        return start, wait, finish

    def publish_rows(ext, piece, start):
        whole = jnp.concatenate([ext[b] for b in range(blocks)], 1)
        for j in range(4):
            picked = jnp.dot(whole, hot[j], preferred_element_type=F32)
            piece[j] = picked.astype(BF16)
            start(j)

    def product(ext, b):
        left = jnp.concatenate([ext[lists[b * kmax + k]] for k in range(kmax)], 1)
        right = jnp.concatenate([trans[b * kmax + k] for k in range(kmax)], 1)
        return lax.dot_general(left, right, LAST, preferred_element_type=F32)

    def bonus(b):
        return jnp.where(gap[...] == b * tile, 1.0, 0.0)

    neighbours = 1
    for by in OFFSETS:
        neighbours = neighbours + inside(by).astype(jnp.int32)
    pl.semaphore_wait(barrier, neighbours)

    start1, wait1, finish1 = exchange(0, piece1, ext1, blocks, -1)
    start2, wait2, finish2 = exchange(1, piece2, ext2, blocks, -1)
    start3, wait3, finish3 = exchange(2, part1, arr1, 0, 1)
    start4, wait4, finish4 = exchange(3, part2, arr2, 0, 1)

    publish_rows(ext1, piece1, start1)

    gap[...] = jnp.broadcast_to(goal[...] - first_seg, (tile, tile)).T - lane
    ids[...] = (routes[...] - first_seg).T
    group = 4

    def count(q, acc):
        highs, lows = [], []
        for g in range(group):
            line = ids[pl.ds(q * group + g, 1), :]
            low = jnp.bitwise_and(line, tile - 1)
            high = lax.shift_right_arithmetic(line, 7)
            lows.append(jnp.where(row == low, 1.0, 0.0).astype(BF16))
            highs.append(jnp.where(row[:blocks] == high, 1.0, 0.0).astype(BF16))
        return acc + lax.dot_general(
            jnp.concatenate(highs, 1), jnp.concatenate(lows, 1), LAST, preferred_element_type=F32
        )

    total[...] = lax.fori_loop(0, ids.shape[0] // group, count, jnp.zeros((blocks, tile), F32))

    load_trans.wait()
    wait1()

    def first_backup(b, carry):
        y = product(ext1, b) + bonus(b)
        ext2[b] = (jnp.exp(reward[pl.ds(b, 1), :]) * y).astype(BF16)
        return carry

    lax.fori_loop(0, blocks, first_backup, 0, unroll=2)
    publish_rows(ext2, piece2, start2)

    load_anchor.wait()

    def turn(b, carry):
        anchor[b] = anchor_in[pl.ds(pl.multiple_of(b * tile, tile), tile), :].astype(F32).T
        return carry

    lax.fori_loop(0, blocks, turn, 0, unroll=2)
    wait2()

    def second_backup(b, carry):
        y = product(ext2, b) + bonus(b)
        w = 1.0 / y
        inv[b] = w
        flow_u[b] = (anchor[b] * w).astype(BF16)
        return carry

    lax.fori_loop(0, blocks, second_backup, 0, unroll=2)

    def spread(part, start):
        def step(t, acc):
            left = jnp.concatenate(
                [flow_u[lists[at_block + 2 * t + h]] for h in range(2)], 1
            )
            right = jnp.concatenate([trans[lists[at_tile + 2 * t + h]] for h in range(2)], 0)
            new = jnp.dot(left, right, preferred_element_type=F32)
            acc = acc * lists[at_keep + t].astype(F32) + new
            sums[t] = acc
            return acc

        lax.fori_loop(0, pairs, step, jnp.zeros((tile, tile), F32), unroll=2)
        for j in range(4):
            part[j] = sums[lists[at_last + blocks + j]].astype(BF16)
            start(j)

    def arrive(arr, c):
        left = jnp.concatenate([arr[j] for j in range(4)], 1)
        rows = pl.ds(pl.multiple_of(c * tile, tile), tile)
        right = jnp.concatenate([hot[j, rows, :] for j in range(4)], 1)
        back = lax.dot_general(left, right, LAST, preferred_element_type=F32)
        local = sums[lists[at_last + c]] + back
        return anchor[c] + ext2[c].astype(F32) * local

    spread(part1, start3)
    wait3()

    def first_flow(c, carry):
        flow = arrive(arr1, c)
        flow_u[c] = (flow * inv[c]).astype(BF16)
        here = pl.ds(c, 1)
        total[here, :] = total[here, :] - jnp.sum(anchor[c] + flow, axis=0, keepdims=True)
        return carry

    lax.fori_loop(0, blocks, first_flow, 0, unroll=2)
    spread(part2, start4)
    wait4()

    def second_flow(c, carry):
        flow = arrive(arr2, c)
        here = pl.ds(c, 1)
        total[here, :] = total[here, :] - jnp.sum(flow, axis=0, keepdims=True)
        return carry

    lax.fori_loop(0, blocks, second_flow, 0, unroll=2)

    share = blocks // 2
    mine = pl.ds(pl.multiple_of(side * share, share), share)
    theirs = pl.ds(pl.multiple_of((1 - side) * share, share), share)
    swap = pltpu.make_async_remote_copy(
        src_ref=total.at[theirs],
        dst_ref=other,
        send_sem=dest_sem.at[0],
        recv_sem=dest_sem.at[1],
        device_id={"dest": 1 - side},
        device_id_type=MESH,
    )
    swap.start()
    finish1()
    finish2()
    finish3()
    finish4()
    swap.wait()
    out[...] = total[mine, :] + other[...]


def body(
    regions,
    transitions,
    tile_cols,
    tile_count,
    publish,
    reward,
    value_init,
    anchor,
    goal_segment_index,
    routes,
):
    blocks, kmax, tile, _ = transitions.shape
    width = anchor.shape[1]
    tiles, cols, pairs = dims(blocks, kmax)
    lists = plan(tile_cols, tile_count)
    vmem = pl.BlockSpec(memory_space=pltpu.VMEM)
    smem = pl.BlockSpec(memory_space=pltpu.SMEM)
    hbm = pl.BlockSpec(memory_space=pl.ANY)
    out = pl.pallas_call(
        functools.partial(kernel, (blocks, kmax, regions)),
        out_shape=jax.ShapeDtypeStruct((blocks // 2, tile), F32),
        in_specs=[smem, vmem, vmem, vmem, vmem, hbm, hbm, hbm],
        out_specs=vmem,
        scratch_shapes=[
            pltpu.VMEM((tiles, tile, tile), BF16),
            pltpu.VMEM((blocks * tile, width), BF16),
            pltpu.VMEM((blocks * tile, width), BF16),
            pltpu.VMEM((blocks, width, tile), F32),
            pltpu.VMEM((cols + 1, width, tile), BF16),
            pltpu.VMEM((cols + 1, width, tile), BF16),
            pltpu.VMEM((4, width, tile), BF16),
            pltpu.VMEM((4, width, tile), BF16),
            pltpu.VMEM((4, blocks * tile, tile), BF16),
            pltpu.VMEM((routes.shape[1], routes.shape[0]), jnp.int32),
            pltpu.VMEM((width, tile), jnp.int32),
            pltpu.VMEM((blocks, width, tile), F32),
            pltpu.VMEM((blocks + 1, width, tile), BF16),
            pltpu.VMEM((pairs + 1, width, tile), F32),
            pltpu.VMEM((4, width, tile), BF16),
            pltpu.VMEM((4, width, tile), BF16),
            pltpu.VMEM((4, width, tile), BF16),
            pltpu.VMEM((4, width, tile), BF16),
            pltpu.VMEM((blocks, tile), F32),
            pltpu.VMEM((blocks // 2, tile), F32),
            pltpu.SemaphoreType.DMA((3,)),
            pltpu.SemaphoreType.DMA((4, 4)),
            pltpu.SemaphoreType.DMA((4, 4)),
            pltpu.SemaphoreType.DMA((2,)),
        ],
        compiler_params=pltpu.CompilerParams(
            collective_id=0, has_side_effects=True, vmem_limit_bytes=40 * 1024 * 1024
        ),
    )(
        lists,
        publish[0],
        reward.reshape(blocks, tile),
        goal_segment_index.reshape(1, width),
        routes,
        transitions.reshape(tiles, tile, tile),
        value_init,
        anchor,
    )
    return out.reshape(-1)


def solution(mesh):
    return jax.shard_map(
        functools.partial(body, mesh.shape["region"]),
        mesh=mesh,
        in_specs=(
            P(("metro", "region"), None, None, None),
            P(("metro", "region"), None),
            P(("metro", "region")),
            P(("metro", "region"), None, None),
            P(("metro", "region")),
            P(("metro", "region"), "dest"),
            P(("metro", "region"), "dest"),
            P(("metro", "dest")),
            P(("metro", "dest"), None),
        ),
        out_specs=P(("metro", "region", "dest")),
        check_vma=False,
    )
```

```python
import functools

import jax
import jax.numpy as jnp
from jax import lax
from jax.experimental import pallas as pl
from jax.experimental.pallas import tpu as pltpu
from jax.sharding import PartitionSpec as P

OFFSETS = (-2, -1, 1, 2)
MESH = pl.DeviceIdType.MESH
F32 = jnp.float32
BF16 = jnp.bfloat16
LAST = (((1,), (1,)), ((), ()))


def dims(blocks, kmax):
    tiles = blocks * kmax
    cols = blocks + 4
    pairs = (tiles + cols) // 2
    return tiles, cols, pairs


def plan(tile_cols, tile_count):
    blocks, kmax = tile_cols.shape
    tiles, cols, pairs = dims(blocks, kmax)
    live = lax.broadcasted_iota(jnp.int32, (blocks, kmax), 1) < tile_count[:, None]
    col = jnp.where(live, tile_cols, cols).reshape(tiles)
    tile = jnp.arange(tiles, dtype=jnp.int32)
    cid = jnp.arange(cols, dtype=jnp.int32)
    same = col[:, None] == col[None, :]
    rank = jnp.sum((same & (tile[None, :] < tile[:, None])).astype(jnp.int32), 1)
    count = jnp.sum((col[:, None] == cid[None, :]).astype(jnp.int32), 0)
    padded = (count + 1) // 2 * 2
    start = jnp.sum(jnp.where(cid[None, :] < cid[:, None], padded[None, :], 0), 1)
    first = jnp.sum(jnp.where(cid[None, :] < col[:, None], padded[None, :], 0), 1)
    spot = jnp.where(col < cols, first + rank, -1)
    slot = jnp.arange(2 * pairs, dtype=jnp.int32)
    hit = slot[:, None] == spot[None, :]
    tile_at = jnp.sum(jnp.where(hit, tile[None, :], 0), 1)
    block_at = blocks + jnp.sum(jnp.where(hit, (tile // kmax - blocks)[None, :], 0), 1)
    pair = jnp.arange(pairs, dtype=jnp.int32)
    fresh = jnp.any((pair[:, None] * 2 == start[None, :]) & (count[None, :] > 0), 1)
    keep = 1 - fresh.astype(jnp.int32)
    last = jnp.where(count > 0, (start + padded) // 2 - 1, pairs)
    return jnp.concatenate([col, tile_at, block_at, keep, last])


def kernel(
    shape,
    lists,
    publish,
    reward,
    goal,
    routes,
    trans_hbm,
    init_hbm,
    anchor_hbm,
    out,
    trans,
    init,
    anchor_in,
    anchor,
    ext1,
    ext2,
    piece1,
    piece2,
    hot,
    ids,
    gap,
    inv,
    flow_u,
    sums,
    part1,
    part2,
    arr1,
    arr2,
    total,
    other,
    load_sem,
    send_sem,
    recv_sem,
    dest_sem,
):
    blocks, kmax, regions = shape
    tiles, cols, pairs = dims(blocks, kmax)
    tile = 128
    me = lax.axis_index("region")
    side = lax.axis_index("dest")
    first_seg = me * (blocks * tile)
    at_tile, at_block = tiles, tiles + 2 * pairs
    at_keep = tiles + 4 * pairs
    at_last = at_keep + pairs

    load_init = pltpu.make_async_copy(init_hbm, init, load_sem.at[0])
    load_trans = pltpu.make_async_copy(trans_hbm, trans, load_sem.at[1])
    load_anchor = pltpu.make_async_copy(anchor_hbm, anchor_in, load_sem.at[2])
    load_init.start()
    load_trans.start()
    load_anchor.start()

    def inside(by):
        return (me + by >= 0) & (me + by < regions)

    barrier = pltpu.get_barrier_semaphore()
    pl.semaphore_signal(barrier, inc=1, device_id={"dest": 1 - side}, device_id_type=MESH)
    for by in OFFSETS:
        @pl.when(inside(by))
        def _():
            pl.semaphore_signal(barrier, inc=1, device_id={"region": me + by}, device_id_type=MESH)

    zero = jnp.zeros((tile, tile), BF16)
    ext1[cols] = zero
    ext2[cols] = zero
    flow_u[blocks] = zero
    sums[pairs] = jnp.zeros((tile, tile), F32)
    for j, by in enumerate(OFFSETS):
        @pl.when(jnp.logical_not(inside(by)))
        def _():
            ext1[blocks + j] = zero
            ext2[blocks + j] = zero

        @pl.when(jnp.logical_not(inside(-by)))
        def _():
            arr1[j] = zero
            arr2[j] = zero

    row = lax.broadcasted_iota(jnp.int32, (tile, tile), 0)
    lane = lax.broadcasted_iota(jnp.int32, (tile, tile), 1)

    def make_hot(c, carry):
        for j in range(4):
            pub = publish[j : j + 1, :]
            hit = (row + c * tile) == pub
            hot[j, pl.ds(pl.multiple_of(c * tile, tile), tile), :] = jnp.where(hit, 1.0, 0.0).astype(BF16)
        return carry

    lax.fori_loop(0, blocks, make_hot, 0, unroll=True)

    load_init.wait()

    def make_start(b, carry):
        block = init[pl.ds(pl.multiple_of(b * tile, tile), tile), :].astype(F32)
        ext1[b] = jnp.exp(block.T).astype(BF16)
        return carry

    lax.fori_loop(0, blocks, make_start, 0, unroll=True)

    def exchange(phase, source, target, base, sign):
        def copy(j):
            return pltpu.make_async_remote_copy(
                src_ref=source.at[j],
                dst_ref=target.at[base + j],
                send_sem=send_sem.at[phase, j],
                recv_sem=recv_sem.at[phase, j],
                device_id={"region": me + sign * OFFSETS[j]},
                device_id_type=MESH,
            )

        def start(j):
            @pl.when(inside(sign * OFFSETS[j]))
            def _():
                copy(j).start()

        def wait():
            for j in range(4):
                @pl.when(inside(-sign * OFFSETS[j]))
                def _():
                    copy(j).wait_recv()

        def finish():
            for j in range(4):
                @pl.when(inside(sign * OFFSETS[j]))
                def _():
                    copy(j).wait_send()

        return start, wait, finish

    def publish_rows(ext, piece, start):
        whole = jnp.concatenate([ext[b] for b in range(blocks)], 1)
        for j in range(4):
            picked = jnp.dot(whole, hot[j], preferred_element_type=F32)
            piece[j] = picked.astype(BF16)
            start(j)

    def product(ext, b):
        left = jnp.concatenate([ext[lists[b * kmax + k]] for k in range(kmax)], 1)
        right = jnp.concatenate([trans[b * kmax + k] for k in range(kmax)], 1)
        return lax.dot_general(left, right, LAST, preferred_element_type=F32)

    def bonus(b):
        return jnp.where(gap[...] == b * tile, 1.0, 0.0)

    neighbours = 1
    for by in OFFSETS:
        neighbours = neighbours + inside(by).astype(jnp.int32)
    pl.semaphore_wait(barrier, neighbours)

    start1, wait1, finish1 = exchange(0, piece1, ext1, blocks, -1)
    start2, wait2, finish2 = exchange(1, piece2, ext2, blocks, -1)
    start3, wait3, finish3 = exchange(2, part1, arr1, 0, 1)
    start4, wait4, finish4 = exchange(3, part2, arr2, 0, 1)

    publish_rows(ext1, piece1, start1)

    gap[...] = jnp.broadcast_to(goal[...] - first_seg, (tile, tile)).T - lane
    ids[...] = routes[...] - first_seg
    group = 4

    def count(q, acc):
        highs, lows = [], []
        for g in range(group):
            line = ids[pl.ds(q * group + g, 1), :]
            low = jnp.bitwise_and(line, tile - 1)
            high = lax.shift_right_arithmetic(line, 7)
            lows.append(jnp.where(row == low, 1.0, 0.0).astype(BF16))
            highs.append(jnp.where(row[:blocks] == high, 1.0, 0.0).astype(BF16))
        return acc + lax.dot_general(
            jnp.concatenate(highs, 1), jnp.concatenate(lows, 1), LAST, preferred_element_type=F32
        )

    total[...] = lax.fori_loop(0, ids.shape[0] // group, count, jnp.zeros((blocks, tile), F32), unroll=True)

    load_trans.wait()
    wait1()

    def first_backup(b, carry):
        y = product(ext1, b) + bonus(b)
        ext2[b] = (jnp.exp(reward[pl.ds(b, 1), :]) * y).astype(BF16)
        return carry

    lax.fori_loop(0, blocks, first_backup, 0, unroll=True)
    publish_rows(ext2, piece2, start2)

    load_anchor.wait()

    def turn(b, carry):
        anchor[b] = anchor_in[pl.ds(pl.multiple_of(b * tile, tile), tile), :].astype(F32).T
        return carry

    lax.fori_loop(0, blocks, turn, 0, unroll=True)
    wait2()

    def second_backup(b, carry):
        y = product(ext2, b) + bonus(b)
        w = 1.0 / y
        inv[b] = w
        flow_u[b] = (anchor[b] * w).astype(BF16)
        return carry

    lax.fori_loop(0, blocks, second_backup, 0, unroll=True)

    def spread(part, start):
        def step(t, acc):
            left = jnp.concatenate(
                [flow_u[lists[at_block + 2 * t + h]] for h in range(2)], 1
            )
            right = jnp.concatenate([trans[lists[at_tile + 2 * t + h]] for h in range(2)], 0)
            new = jnp.dot(left, right, preferred_element_type=F32)
            acc = acc * lists[at_keep + t].astype(F32) + new
            sums[t] = acc
            return acc

        lax.fori_loop(0, pairs, step, jnp.zeros((tile, tile), F32), unroll=True)
        for j in range(4):
            part[j] = sums[lists[at_last + blocks + j]].astype(BF16)
            start(j)

    def arrive(arr, c):
        left = jnp.concatenate([arr[j] for j in range(4)], 1)
        rows = pl.ds(pl.multiple_of(c * tile, tile), tile)
        right = jnp.concatenate([hot[j, rows, :] for j in range(4)], 1)
        back = lax.dot_general(left, right, LAST, preferred_element_type=F32)
        local = sums[lists[at_last + c]] + back
        return anchor[c] + ext2[c].astype(F32) * local

    spread(part1, start3)
    wait3()

    def first_flow(c, carry):
        flow = arrive(arr1, c)
        flow_u[c] = (flow * inv[c]).astype(BF16)
        here = pl.ds(c, 1)
        total[here, :] = total[here, :] - jnp.sum(anchor[c] + flow, axis=0, keepdims=True)
        return carry

    lax.fori_loop(0, blocks, first_flow, 0, unroll=True)
    spread(part2, start4)
    wait4()

    def second_flow(c, carry):
        flow = arrive(arr2, c)
        here = pl.ds(c, 1)
        total[here, :] = total[here, :] - jnp.sum(flow, axis=0, keepdims=True)
        return carry

    lax.fori_loop(0, blocks, second_flow, 0, unroll=True)

    share = blocks // 2
    mine = pl.ds(pl.multiple_of(side * share, share), share)
    theirs = pl.ds(pl.multiple_of((1 - side) * share, share), share)
    swap = pltpu.make_async_remote_copy(
        src_ref=total.at[theirs],
        dst_ref=other,
        send_sem=dest_sem.at[0],
        recv_sem=dest_sem.at[1],
        device_id={"dest": 1 - side},
        device_id_type=MESH,
    )
    swap.start()
    finish1()
    finish2()
    finish3()
    finish4()
    swap.wait()
    out[...] = total[mine, :] + other[...]


def body(
    regions,
    transitions,
    tile_cols,
    tile_count,
    publish,
    reward,
    value_init,
    anchor,
    goal_segment_index,
    routes,
):
    blocks, kmax, tile, _ = transitions.shape
    width = anchor.shape[1]
    tiles, cols, pairs = dims(blocks, kmax)
    lists = plan(tile_cols, tile_count)
    vmem = pl.BlockSpec(memory_space=pltpu.VMEM)
    smem = pl.BlockSpec(memory_space=pltpu.SMEM)
    hbm = pl.BlockSpec(memory_space=pltpu.HBM)
    out = pl.pallas_call(
        functools.partial(kernel, (blocks, kmax, regions)),
        out_shape=jax.ShapeDtypeStruct((blocks // 2, tile), F32),
        in_specs=[smem, vmem, vmem, vmem, vmem, hbm, hbm, hbm],
        out_specs=vmem,
        scratch_shapes=[
            pltpu.VMEM((tiles, tile, tile), BF16),
            pltpu.VMEM((blocks * tile, width), BF16),
            pltpu.VMEM((blocks * tile, width), BF16),
            pltpu.VMEM((blocks, width, tile), F32),
            pltpu.VMEM((cols + 1, width, tile), BF16),
            pltpu.VMEM((cols + 1, width, tile), BF16),
            pltpu.VMEM((4, width, tile), BF16),
            pltpu.VMEM((4, width, tile), BF16),
            pltpu.VMEM((4, blocks * tile, tile), BF16),
            pltpu.VMEM((routes.shape[1], routes.shape[0]), jnp.int32),
            pltpu.VMEM((width, tile), jnp.int32),
            pltpu.VMEM((blocks, width, tile), F32),
            pltpu.VMEM((blocks + 1, width, tile), BF16),
            pltpu.VMEM((pairs + 1, width, tile), F32),
            pltpu.VMEM((4, width, tile), BF16),
            pltpu.VMEM((4, width, tile), BF16),
            pltpu.VMEM((4, width, tile), BF16),
            pltpu.VMEM((4, width, tile), BF16),
            pltpu.VMEM((blocks, tile), F32),
            pltpu.VMEM((blocks // 2, tile), F32),
            pltpu.SemaphoreType.DMA((3,)),
            pltpu.SemaphoreType.DMA((4, 4)),
            pltpu.SemaphoreType.DMA((4, 4)),
            pltpu.SemaphoreType.DMA((2,)),
        ],
        compiler_params=pltpu.CompilerParams(
            collective_id=0, has_side_effects=True, vmem_limit_bytes=56 * 1024 * 1024
        ),
    )(
        lists,
        publish[0],
        reward.reshape(blocks, tile),
        goal_segment_index.reshape(1, width),
        routes.T,
        transitions.reshape(tiles, tile, tile),
        value_init,
        anchor,
    )
    return out.reshape(-1)


def solution(mesh):
    return jax.shard_map(
        functools.partial(body, mesh.shape["region"]),
        mesh=mesh,
        in_specs=(
            P(("metro", "region"), None, None, None),
            P(("metro", "region"), None),
            P(("metro", "region")),
            P(("metro", "region"), None, None),
            P(("metro", "region")),
            P(("metro", "region"), "dest"),
            P(("metro", "region"), "dest"),
            P(("metro", "dest")),
            P(("metro", "dest"), None),
        ),
        out_specs=P(("metro", "region", "dest")),
        check_vma=False,
    )
```

```python
import functools

import jax
import jax.numpy as jnp
from jax import lax
from jax.experimental import pallas as pl
from jax.experimental.pallas import tpu as pltpu
from jax.sharding import PartitionSpec as P

OFFSETS = (-2, -1, 1, 2)
ORDER = (1, 2, 0, 3)
MESH = pl.DeviceIdType.MESH
F32 = jnp.float32
BF16 = jnp.bfloat16
LAST = (((1,), (1,)), ((), ()))


def dims(blocks, kmax):
    tiles = blocks * kmax
    cols = blocks + 4
    pairs = (tiles + cols) // 2
    return tiles, cols, pairs


def plan(tile_cols, tile_count):
    blocks, kmax = tile_cols.shape
    tiles, cols, _ = dims(blocks, kmax)
    live = lax.broadcasted_iota(jnp.int32, (blocks, kmax), 1) < tile_count[:, None]
    col = jnp.where(live, tile_cols, cols).reshape(1, tiles)
    return jnp.pad(col, ((0, 0), (0, 128 - tiles)), constant_values=cols)


def make_lists(col, row, lane, shape):
    blocks, kmax = shape
    tiles, cols, pairs = dims(blocks, kmax)

    def down(x):
        return jnp.sum(x, axis=0, keepdims=True)

    def across(x):
        return jnp.sum(x, axis=1, keepdims=True)

    col = jnp.where(lane[:1] < tiles, col, cols)
    by_lane = jnp.broadcast_to(col, row.shape)
    by_row = by_lane.T
    rank = down(jnp.where((by_lane == by_row) & (row < lane), 1, 0))
    count_row = down(jnp.where((by_row == lane) & (lane < cols), 1, 0))
    count_col = across(jnp.where((by_lane == row) & (row < cols), 1, 0))
    padded_row = jnp.bitwise_and(count_row + 1, -2)
    padded_col = jnp.bitwise_and(count_col + 1, -2)
    start_row = down(jnp.where(row < lane, padded_col, 0))
    start_col = across(jnp.where(lane < row, padded_row, 0))
    first = down(jnp.where(row < by_lane, padded_col, 0))
    spot = jnp.where(col < cols, first + rank, -1)
    hit = jnp.broadcast_to(spot, row.shape).T == lane
    tile_at = down(jnp.where(hit, row, 0))
    owner = lax.shift_right_logical(row * (256 // kmax + 1), 8)
    block_at = blocks + down(jnp.where(hit, owner - blocks, 0))
    keep = 1 - down(jnp.where((start_col == 2 * lane) & (count_col > 0), 1, 0))
    last = jnp.where(count_row > 0, lax.shift_right_logical(start_row + padded_row, 1) - 1, pairs)
    return jnp.concatenate([col, tile_at, block_at, keep, last, col, col, col], 0)


def kernel(
    shape,
    columns,
    publish,
    reward,
    goal,
    routes,
    trans_hbm,
    init_hbm,
    anchor_hbm,
    out,
    trans,
    init,
    anchor_in,
    anchor,
    ext1,
    ext2,
    piece1,
    piece2,
    hot,
    ids,
    gap,
    inv,
    flow_u,
    sums,
    part1,
    arr1,
    total,
    other,
    terms,
    away,
    table,
    lists,
    load_sem,
    send_sem,
    recv_sem,
    dest_sem,
    terms_send,
    terms_recv,
):
    blocks, kmax, regions = shape
    tiles, cols, pairs = dims(blocks, kmax)
    tile = 128
    me = lax.axis_index("region")
    side = lax.axis_index("dest")
    first_seg = me * (blocks * tile)
    of_col, of_tile, of_block, of_keep, of_last = range(5)

    load_init = pltpu.make_async_copy(init_hbm, init, load_sem.at[0])
    load_trans = pltpu.make_async_copy(trans_hbm, trans, load_sem.at[1])
    load_anchor = pltpu.make_async_copy(anchor_hbm, anchor_in, load_sem.at[2])
    load_init.start()
    load_trans.start()
    load_anchor.start()

    def inside(by):
        return (me + by >= 0) & (me + by < regions)

    barrier = pltpu.get_barrier_semaphore()
    pl.semaphore_signal(barrier, inc=1, device_id={"dest": 1 - side}, device_id_type=MESH)
    for by in OFFSETS:
        @pl.when(inside(by))
        def _():
            for d in range(2):
                pl.semaphore_signal(barrier, inc=1, device_id={"region": me + by, "dest": d}, device_id_type=MESH)

    zero = jnp.zeros((tile, tile), BF16)
    ext1[cols] = zero
    ext2[cols] = zero
    flow_u[blocks] = zero
    sums[pairs] = jnp.zeros((tile, tile), F32)
    for j, by in enumerate(OFFSETS):
        @pl.when(jnp.logical_not(inside(by)))
        def _():
            ext1[blocks + j] = zero
            ext2[blocks + j] = zero

        @pl.when(jnp.logical_not(inside(-by)))
        def _():
            arr1[j] = zero
            for d in range(2):
                away[d, j] = jnp.zeros((8, tile), F32)

    row = lax.broadcasted_iota(jnp.int32, (tile, tile), 0)
    lane = lax.broadcasted_iota(jnp.int32, (tile, tile), 1)

    def make_hot(c, carry):
        for j in range(4):
            pub = publish[j : j + 1, :]
            hit = (row + c * tile) == pub
            hot[j, pl.ds(pl.multiple_of(c * tile, tile), tile), :] = jnp.where(hit, 1.0, 0.0).astype(BF16)
        return carry

    lax.fori_loop(0, blocks, make_hot, 0, unroll=True)

    load_init.wait()

    def make_start(b, carry):
        block = init[pl.ds(pl.multiple_of(b * tile, tile), tile), :].astype(F32)
        ext1[b] = jnp.exp(block.T).astype(BF16)
        return carry

    lax.fori_loop(0, blocks, make_start, 0, unroll=True)

    def exchange(phase, source, target, base, sign):
        def copy(j):
            return pltpu.make_async_remote_copy(
                src_ref=source.at[j],
                dst_ref=target.at[base + j],
                send_sem=send_sem.at[phase, j],
                recv_sem=recv_sem.at[phase, j],
                device_id={"region": me + sign * OFFSETS[j]},
                device_id_type=MESH,
            )

        def start(j):
            @pl.when(inside(sign * OFFSETS[j]))
            def _():
                copy(j).start()

        def wait():
            for j in range(4):
                @pl.when(inside(-sign * OFFSETS[j]))
                def _():
                    copy(j).wait_recv()

        def finish():
            for j in range(4):
                @pl.when(inside(sign * OFFSETS[j]))
                def _():
                    copy(j).wait_send()

        return start, wait, finish

    def publish_rows(ext, piece, start):
        whole = jnp.concatenate([ext[b] for b in range(blocks)], 1)
        for j in ORDER:
            picked = jnp.dot(whole, hot[j], preferred_element_type=F32)
            piece[j] = picked.astype(BF16)
            start(j)

    def product(ext, b):
        left = jnp.concatenate([ext[lists[of_col, b * kmax + k]] for k in range(kmax)], 1)
        right = jnp.concatenate([trans[b * kmax + k] for k in range(kmax)], 1)
        return lax.dot_general(left, right, LAST, preferred_element_type=F32)

    def bonus(b):
        return jnp.where(gap[...] == b * tile, 1.0, 0.0)

    neighbours = 1
    for by in OFFSETS:
        neighbours = neighbours + 2 * inside(by).astype(jnp.int32)
    pl.semaphore_wait(barrier, neighbours)

    start1, wait1, finish1 = exchange(0, piece1, ext1, blocks, -1)
    start2, wait2, finish2 = exchange(1, piece2, ext2, blocks, -1)
    start3, wait3, finish3 = exchange(2, part1, arr1, 0, 1)

    publish_rows(ext1, piece1, start1)

    gap[...] = jnp.broadcast_to(goal[...] - first_seg, (tile, tile)).T - lane
    ids[...] = routes[...] - first_seg
    group = 4

    def count(q, acc):
        highs, lows = [], []
        for g in range(group):
            line = ids[pl.ds(q * group + g, 1), :]
            low = jnp.bitwise_and(line, tile - 1)
            high = lax.shift_right_arithmetic(line, 7)
            lows.append(jnp.where(row == low, 1.0, 0.0).astype(BF16))
            highs.append(jnp.where(row[:blocks] == high, 1.0, 0.0).astype(BF16))
        return acc + lax.dot_general(
            jnp.concatenate(highs, 1), jnp.concatenate(lows, 1), LAST, preferred_element_type=F32
        )

    table[...] = make_lists(columns[...], row, lane, (blocks, kmax))
    load_lists = pltpu.make_async_copy(table, lists, load_sem.at[3])
    load_lists.start()
    groups = ids.shape[0] // group
    counted = lax.fori_loop(0, groups // 2, count, jnp.zeros((blocks, tile), F32), unroll=True)
    load_lists.wait()
    load_trans.wait()
    wait1()

    def first_backup(b, carry):
        y = product(ext1, b) + bonus(b)
        ext2[b] = (jnp.exp(reward[pl.ds(b, 1), :]) * y).astype(BF16)
        return carry

    lax.fori_loop(0, blocks, first_backup, 0, unroll=True)
    publish_rows(ext2, piece2, start2)

    load_anchor.wait()

    def turn(b, carry):
        anchor[b] = anchor_in[pl.ds(pl.multiple_of(b * tile, tile), tile), :].astype(F32).T
        return carry

    lax.fori_loop(0, blocks, turn, 0, unroll=True)
    total[...] = lax.fori_loop(groups // 2, groups, count, counted, unroll=True)
    wait2()

    def second_backup(b, carry):
        y = product(ext2, b) + bonus(b)
        w = 1.0 / y
        inv[b] = w
        flow_u[b] = (anchor[b] * w).astype(BF16)
        return carry

    lax.fori_loop(0, blocks, second_backup, 0, unroll=True)

    def spread():
        def step(t, acc):
            left = jnp.concatenate(
                [flow_u[lists[of_block, 2 * t + h]] for h in range(2)], 1
            )
            right = jnp.concatenate([trans[lists[of_tile, 2 * t + h]] for h in range(2)], 0)
            new = jnp.dot(left, right, preferred_element_type=F32)
            acc = acc * lists[of_keep, t].astype(F32) + new
            sums[t] = acc
            return acc

        lax.fori_loop(0, pairs, step, jnp.zeros((tile, tile), F32), unroll=True)

    def arrive(arr, c):
        left = jnp.concatenate([arr[j] for j in range(4)], 1)
        rows = pl.ds(pl.multiple_of(c * tile, tile), tile)
        right = jnp.concatenate([hot[j, rows, :] for j in range(4)], 1)
        back = lax.dot_general(left, right, LAST, preferred_element_type=F32)
        local = sums[lists[of_last, c]] + back
        return anchor[c] + ext2[c].astype(F32) * local

    spread()
    for j in ORDER:
        part1[j] = sums[lists[of_last, blocks + j]].astype(BF16)
        start3(j)
    wait3()

    def first_flow(c, carry):
        flow = arrive(arr1, c)
        flow_u[c] = (flow * inv[c]).astype(BF16)
        here = pl.ds(c, 1)
        total[here, :] = total[here, :] - jnp.sum(anchor[c] + flow, axis=0, keepdims=True)
        return carry

    lax.fori_loop(0, blocks, first_flow, 0, unroll=True)
    spread()

    def term_copy(j, d, slot):
        return pltpu.make_async_remote_copy(
            src_ref=terms.at[j],
            dst_ref=away.at[slot, j],
            send_sem=terms_send.at[d, j],
            recv_sem=terms_recv.at[slot, j],
            device_id={"region": me + OFFSETS[j], "dest": d},
            device_id_type=MESH,
        )

    for j in ORDER:
        flow = sums[lists[of_last, blocks + j]] * ext2[blocks + j].astype(F32)
        terms[j] = jnp.sum(flow.reshape(tile // 8, 8, tile), axis=0)

        @pl.when(inside(OFFSETS[j]))
        def _():
            for d in range(2):
                term_copy(j, d, side).start()

    def second_flow(c, carry):
        flow = anchor[c] + ext2[c].astype(F32) * sums[lists[of_last, c]]
        here = pl.ds(c, 1)
        total[here, :] = total[here, :] - jnp.sum(flow, axis=0, keepdims=True)
        return carry

    lax.fori_loop(0, blocks, second_flow, 0, unroll=True)

    share = blocks // 2
    mine = pl.ds(pl.multiple_of(side * share, share), share)
    theirs = pl.ds(pl.multiple_of((1 - side) * share, share), share)
    swap = pltpu.make_async_remote_copy(
        src_ref=total.at[theirs],
        dst_ref=other,
        send_sem=dest_sem.at[0],
        recv_sem=dest_sem.at[1],
        device_id={"dest": 1 - side},
        device_id_type=MESH,
    )
    swap.start()
    finish1()
    finish2()
    finish3()
    for j in range(4):
        @pl.when(inside(OFFSETS[j]))
        def _():
            for d in range(2):
                term_copy(j, d, side).wait_send()

        @pl.when(inside(-OFFSETS[j]))
        def _():
            for d in range(2):
                term_copy(j, d, d).wait_recv()

    whole = jnp.concatenate([away[0, j] + away[1, j] for j in range(4)], 1)
    high = whole.astype(BF16)
    rest = whole - high.astype(F32)
    middle = rest.astype(BF16)
    low = (rest - middle.astype(F32)).astype(BF16)
    left = jnp.concatenate([high, middle, low, jnp.zeros_like(low)], 0)
    lines = []
    for i in range(share):
        rows = pl.ds(pl.multiple_of((side * share + i) * tile, tile), tile)
        right = jnp.concatenate([hot[j, rows, :] for j in range(4)], 1)
        back = lax.dot_general(left, right, LAST, preferred_element_type=F32)
        lines.append(jnp.sum(back, axis=0, keepdims=True))
    landed = jnp.concatenate(lines, 0)
    swap.wait()
    out[...] = total[mine, :] + other[...] - landed


def body(
    regions,
    transitions,
    tile_cols,
    tile_count,
    publish,
    reward,
    value_init,
    anchor,
    goal_segment_index,
    routes,
):
    blocks, kmax, tile, _ = transitions.shape
    width = anchor.shape[1]
    tiles, cols, pairs = dims(blocks, kmax)
    columns = plan(tile_cols, tile_count)
    vmem = pl.BlockSpec(memory_space=pltpu.VMEM)
    hbm = pl.BlockSpec(memory_space=pltpu.HBM)
    out = pl.pallas_call(
        functools.partial(kernel, (blocks, kmax, regions)),
        out_shape=jax.ShapeDtypeStruct((blocks // 2, tile), F32),
        in_specs=[vmem, vmem, vmem, vmem, vmem, hbm, hbm, hbm],
        out_specs=vmem,
        scratch_shapes=[
            pltpu.VMEM((tiles, tile, tile), BF16),
            pltpu.VMEM((blocks * tile, width), BF16),
            pltpu.VMEM((blocks * tile, width), BF16),
            pltpu.VMEM((blocks, width, tile), F32),
            pltpu.VMEM((cols + 1, width, tile), BF16),
            pltpu.VMEM((cols + 1, width, tile), BF16),
            pltpu.VMEM((4, width, tile), BF16),
            pltpu.VMEM((4, width, tile), BF16),
            pltpu.VMEM((4, blocks * tile, tile), BF16),
            pltpu.VMEM((routes.shape[1], routes.shape[0]), jnp.int32),
            pltpu.VMEM((width, tile), jnp.int32),
            pltpu.VMEM((blocks, width, tile), F32),
            pltpu.VMEM((blocks + 1, width, tile), BF16),
            pltpu.VMEM((pairs + 1, width, tile), F32),
            pltpu.VMEM((4, width, tile), BF16),
            pltpu.VMEM((4, width, tile), BF16),
            pltpu.VMEM((blocks, tile), F32),
            pltpu.VMEM((blocks // 2, tile), F32),
            pltpu.VMEM((4, 8, tile), F32),
            pltpu.VMEM((2, 4, 8, tile), F32),
            pltpu.VMEM((8, 128), jnp.int32),
            pltpu.SMEM((8, 128), jnp.int32),
            pltpu.SemaphoreType.DMA((4,)),
            pltpu.SemaphoreType.DMA((3, 4)),
            pltpu.SemaphoreType.DMA((3, 4)),
            pltpu.SemaphoreType.DMA((2,)),
            pltpu.SemaphoreType.DMA((2, 4)),
            pltpu.SemaphoreType.DMA((2, 4)),
        ],
        compiler_params=pltpu.CompilerParams(
            collective_id=0, has_side_effects=True, vmem_limit_bytes=56 * 1024 * 1024
        ),
    )(
        columns,
        publish[0],
        reward.reshape(blocks, tile),
        goal_segment_index.reshape(1, width),
        routes.T,
        transitions.reshape(tiles, tile, tile),
        value_init,
        anchor,
    )
    return out.reshape(-1)


def solution(mesh):
    return jax.shard_map(
        functools.partial(body, mesh.shape["region"]),
        mesh=mesh,
        in_specs=(
            P(("metro", "region"), None, None, None),
            P(("metro", "region"), None),
            P(("metro", "region")),
            P(("metro", "region"), None, None),
            P(("metro", "region")),
            P(("metro", "region"), "dest"),
            P(("metro", "region"), "dest"),
            P(("metro", "dest")),
            P(("metro", "dest"), None),
        ),
        out_specs=P(("metro", "region", "dest")),
        check_vma=False,
    )
```

```python
import functools

import jax
import jax.numpy as jnp
from jax import lax
from jax.experimental import pallas as pl
from jax.experimental.pallas import tpu as pltpu
from jax.sharding import PartitionSpec as P

OFFSETS = (-2, -1, 1, 2)
ORDER = (1, 2, 0, 3)
MESH = pl.DeviceIdType.MESH
F32 = jnp.float32
BF16 = jnp.bfloat16
LAST = (((1,), (1,)), ((), ()))


def dims(blocks, kmax):
    tiles = blocks * kmax
    cols = blocks + 4
    pairs = (tiles + cols) // 2
    return tiles, cols, pairs


def plan(tile_cols, tile_count):
    blocks, kmax = tile_cols.shape
    tiles, cols, _ = dims(blocks, kmax)
    live = lax.broadcasted_iota(jnp.int32, (blocks, kmax), 1) < tile_count[:, None]
    col = jnp.where(live, tile_cols, cols).reshape(1, tiles)
    return jnp.pad(col, ((0, 0), (0, 128 - tiles)), constant_values=cols)


def make_lists(col, row, lane, shape):
    blocks, kmax = shape
    tiles, cols, pairs = dims(blocks, kmax)

    def down(x):
        return jnp.sum(x, axis=0, keepdims=True)

    def across(x):
        return jnp.sum(x, axis=1, keepdims=True)

    col = jnp.where(lane[:1] < tiles, col, cols)
    by_lane = jnp.broadcast_to(col, row.shape)
    by_row = by_lane.T
    rank = down(jnp.where((by_lane == by_row) & (row < lane), 1, 0))
    count_row = down(jnp.where((by_row == lane) & (lane < cols), 1, 0))
    count_col = across(jnp.where((by_lane == row) & (row < cols), 1, 0))
    padded_row = jnp.bitwise_and(count_row + 1, -2)
    padded_col = jnp.bitwise_and(count_col + 1, -2)
    start_row = down(jnp.where(row < lane, padded_col, 0))
    start_col = across(jnp.where(lane < row, padded_row, 0))
    first = down(jnp.where(row < by_lane, padded_col, 0))
    spot = jnp.where(col < cols, first + rank, -1)
    hit = jnp.broadcast_to(spot, row.shape).T == lane
    tile_at = down(jnp.where(hit, row, 0))
    owner = lax.shift_right_logical(row * (256 // kmax + 1), 8)
    block_at = blocks + down(jnp.where(hit, owner - blocks, 0))
    keep = 1 - down(jnp.where((start_col == 2 * lane) & (count_col > 0), 1, 0))
    last = jnp.where(count_row > 0, lax.shift_right_logical(start_row + padded_row, 1) - 1, pairs)
    return jnp.concatenate([col, tile_at, block_at, keep, last, col, col, col], 0)


def kernel(
    shape,
    columns,
    publish,
    reward,
    goal,
    routes,
    trans_hbm,
    init_hbm,
    anchor_hbm,
    out,
    out_less,
    trans,
    init,
    anchor_in,
    anchor,
    ext1,
    ext2,
    piece1,
    piece2,
    hot,
    ids,
    gap,
    inv,
    flow_u,
    sums,
    part1,
    arr1,
    total,
    other,
    terms,
    away,
    table,
    lists,
    load_sem,
    send_sem,
    recv_sem,
    dest_sem,
    terms_send,
    terms_recv,
):
    blocks, kmax, regions = shape
    tiles, cols, pairs = dims(blocks, kmax)
    tile = 128
    me = lax.axis_index("region")
    side = lax.axis_index("dest")
    first_seg = me * (blocks * tile)
    of_col, of_tile, of_block, of_keep, of_last = range(5)

    load_init = pltpu.make_async_copy(init_hbm, init, load_sem.at[0])
    load_trans = pltpu.make_async_copy(trans_hbm, trans, load_sem.at[1])
    load_anchor = pltpu.make_async_copy(anchor_hbm, anchor_in, load_sem.at[2])
    load_init.start()
    load_trans.start()
    load_anchor.start()

    def inside(by):
        return (me + by >= 0) & (me + by < regions)

    barrier = pltpu.get_barrier_semaphore()
    pl.semaphore_signal(barrier, inc=1, device_id={"dest": 1 - side}, device_id_type=MESH)
    for by in OFFSETS:
        @pl.when(inside(by))
        def _():
            for d in range(2):
                pl.semaphore_signal(barrier, inc=1, device_id={"region": me + by, "dest": d}, device_id_type=MESH)

    zero = jnp.zeros((tile, tile), BF16)
    ext1[cols] = zero
    ext2[cols] = zero
    flow_u[blocks] = zero
    sums[pairs] = jnp.zeros((tile, tile), F32)
    for j, by in enumerate(OFFSETS):
        @pl.when(jnp.logical_not(inside(by)))
        def _():
            ext1[blocks + j] = zero
            ext2[blocks + j] = zero

        @pl.when(jnp.logical_not(inside(-by)))
        def _():
            arr1[j] = zero
            for d in range(2):
                away[d, j] = jnp.zeros((8, tile), F32)

    row = lax.broadcasted_iota(jnp.int32, (tile, tile), 0)
    lane = lax.broadcasted_iota(jnp.int32, (tile, tile), 1)

    def make_hot(c, carry):
        for j in range(4):
            pub = publish[j : j + 1, :]
            hit = (row + c * tile) == pub
            hot[j, pl.ds(pl.multiple_of(c * tile, tile), tile), :] = jnp.where(hit, 1.0, 0.0).astype(BF16)
        return carry

    lax.fori_loop(0, blocks, make_hot, 0, unroll=True)

    load_init.wait()

    def make_start(b, carry):
        block = init[pl.ds(pl.multiple_of(b * tile, tile), tile), :].astype(F32)
        ext1[b] = jnp.exp(block.T).astype(BF16)
        return carry

    lax.fori_loop(0, blocks, make_start, 0, unroll=True)

    def exchange(phase, source, target, base, sign):
        def copy(j):
            return pltpu.make_async_remote_copy(
                src_ref=source.at[j],
                dst_ref=target.at[base + j],
                send_sem=send_sem.at[phase, j],
                recv_sem=recv_sem.at[phase, j],
                device_id={"region": me + sign * OFFSETS[j]},
                device_id_type=MESH,
            )

        def start(j):
            @pl.when(inside(sign * OFFSETS[j]))
            def _():
                copy(j).start()

        def wait():
            for j in range(4):
                @pl.when(inside(-sign * OFFSETS[j]))
                def _():
                    copy(j).wait_recv()

        def finish():
            for j in range(4):
                @pl.when(inside(sign * OFFSETS[j]))
                def _():
                    copy(j).wait_send()

        return start, wait, finish

    def publish_rows(ext, piece, start):
        whole = jnp.concatenate([ext[b] for b in range(blocks)], 1)
        for j in ORDER:
            picked = jnp.dot(whole, hot[j], preferred_element_type=F32)
            piece[j] = picked.astype(BF16)
            start(j)

    def product(ext, b):
        left = jnp.concatenate([ext[lists[of_col, b * kmax + k]] for k in range(kmax)], 1)
        right = jnp.concatenate([trans[b * kmax + k] for k in range(kmax)], 1)
        return lax.dot_general(left, right, LAST, preferred_element_type=F32)

    def bonus(b):
        return jnp.where(gap[...] == b * tile, 1.0, 0.0)

    neighbours = 1
    for by in OFFSETS:
        neighbours = neighbours + 2 * inside(by).astype(jnp.int32)
    pl.semaphore_wait(barrier, neighbours)

    start1, wait1, finish1 = exchange(0, piece1, ext1, blocks, -1)
    start2, wait2, finish2 = exchange(1, piece2, ext2, blocks, -1)
    start3, wait3, finish3 = exchange(2, part1, arr1, 0, 1)

    publish_rows(ext1, piece1, start1)

    gap[...] = jnp.broadcast_to(goal[...] - first_seg, (tile, tile)).T - lane
    ids[...] = routes[...] - first_seg
    group = 4

    def count(q, acc):
        highs, lows = [], []
        for g in range(group):
            line = ids[pl.ds(q * group + g, 1), :]
            low = jnp.bitwise_and(line, tile - 1)
            high = lax.shift_right_arithmetic(line, 7)
            lows.append(jnp.where(row == low, 1.0, 0.0).astype(BF16))
            highs.append(jnp.where(row[:blocks] == high, 1.0, 0.0).astype(BF16))
        return acc + lax.dot_general(
            jnp.concatenate(highs, 1), jnp.concatenate(lows, 1), LAST, preferred_element_type=F32
        )

    table[...] = make_lists(columns[...], row, lane, (blocks, kmax))
    load_lists = pltpu.make_async_copy(table, lists, load_sem.at[3])
    load_lists.start()
    groups = ids.shape[0] // group
    counted = lax.fori_loop(0, groups // 2, count, jnp.zeros((blocks, tile), F32), unroll=True)
    load_lists.wait()
    load_trans.wait()
    wait1()

    def first_backup(b, carry):
        y = product(ext1, b) + bonus(b)
        ext2[b] = (jnp.exp(reward[pl.ds(b, 1), :]) * y).astype(BF16)
        return carry

    lax.fori_loop(0, blocks, first_backup, 0, unroll=True)
    publish_rows(ext2, piece2, start2)

    load_anchor.wait()

    def turn(b, carry):
        anchor[b] = anchor_in[pl.ds(pl.multiple_of(b * tile, tile), tile), :].astype(F32).T
        return carry

    lax.fori_loop(0, blocks, turn, 0, unroll=True)
    total[...] = lax.fori_loop(groups // 2, groups, count, counted, unroll=True)
    wait2()

    def second_backup(b, carry):
        y = product(ext2, b) + bonus(b)
        w = 1.0 / y
        inv[b] = w
        flow_u[b] = (anchor[b] * w).astype(BF16)
        return carry

    lax.fori_loop(0, blocks, second_backup, 0, unroll=True)

    def spread():
        def step(t, acc):
            left = jnp.concatenate(
                [flow_u[lists[of_block, 2 * t + h]] for h in range(2)], 1
            )
            right = jnp.concatenate([trans[lists[of_tile, 2 * t + h]] for h in range(2)], 0)
            new = jnp.dot(left, right, preferred_element_type=F32)
            acc = acc * lists[of_keep, t].astype(F32) + new
            sums[t] = acc
            return acc

        lax.fori_loop(0, pairs, step, jnp.zeros((tile, tile), F32), unroll=True)

    def arrive(arr, c):
        left = jnp.concatenate([arr[j] for j in range(4)], 1)
        rows = pl.ds(pl.multiple_of(c * tile, tile), tile)
        right = jnp.concatenate([hot[j, rows, :] for j in range(4)], 1)
        back = lax.dot_general(left, right, LAST, preferred_element_type=F32)
        local = sums[lists[of_last, c]] + back
        return anchor[c] + ext2[c].astype(F32) * local

    spread()
    for j in ORDER:
        part1[j] = sums[lists[of_last, blocks + j]].astype(BF16)
        start3(j)
    wait3()

    def first_flow(c, carry):
        flow = arrive(arr1, c)
        flow_u[c] = (flow * inv[c]).astype(BF16)
        here = pl.ds(c, 1)
        total[here, :] = total[here, :] - jnp.sum(anchor[c] + flow, axis=0, keepdims=True)
        return carry

    lax.fori_loop(0, blocks, first_flow, 0, unroll=True)
    spread()

    def term_copy(j, d, slot):
        return pltpu.make_async_remote_copy(
            src_ref=terms.at[j],
            dst_ref=away.at[slot, j],
            send_sem=terms_send.at[d, j],
            recv_sem=terms_recv.at[slot, j],
            device_id={"region": me + OFFSETS[j], "dest": d},
            device_id_type=MESH,
        )

    for j in ORDER:
        flow = sums[lists[of_last, blocks + j]] * ext2[blocks + j].astype(F32)
        terms[j] = jnp.sum(flow.reshape(tile // 8, 8, tile), axis=0)

        @pl.when(inside(OFFSETS[j]))
        def _():
            for d in range(2):
                term_copy(j, d, side).start()

    def second_flow(c, carry):
        flow = anchor[c] + ext2[c].astype(F32) * sums[lists[of_last, c]]
        here = pl.ds(c, 1)
        total[here, :] = total[here, :] - jnp.sum(flow, axis=0, keepdims=True)
        return carry

    lax.fori_loop(0, blocks, second_flow, 0, unroll=True)

    share = blocks // 2
    mine = pl.ds(pl.multiple_of(side * share, share), share)
    theirs = pl.ds(pl.multiple_of((1 - side) * share, share), share)
    swap = pltpu.make_async_remote_copy(
        src_ref=total.at[theirs],
        dst_ref=other,
        send_sem=dest_sem.at[0],
        recv_sem=dest_sem.at[1],
        device_id={"dest": 1 - side},
        device_id_type=MESH,
    )
    swap.start()
    finish1()
    finish2()
    finish3()
    for j in range(4):
        @pl.when(inside(OFFSETS[j]))
        def _():
            for d in range(2):
                term_copy(j, d, side).wait_send()

        @pl.when(inside(-OFFSETS[j]))
        def _():
            for d in range(2):
                term_copy(j, d, d).wait_recv()

    whole = jnp.concatenate([away[0, j] + away[1, j] for j in range(4)], 1)
    high = whole.astype(BF16)
    rest = whole - high.astype(F32)
    middle = rest.astype(BF16)
    low = (rest - middle.astype(F32)).astype(BF16)
    left = jnp.concatenate([high, middle, low, jnp.zeros_like(low)], 0)
    lines = []
    for i in range(share):
        rows = pl.ds(pl.multiple_of((side * share + i) * tile, tile), tile)
        right = jnp.concatenate([hot[j, rows, :] for j in range(4)], 1)
        back = lax.dot_general(left, right, LAST, preferred_element_type=F32)
        lines.append(jnp.sum(back, axis=0, keepdims=True))
    landed = jnp.concatenate(lines, 0)
    swap.wait()
    out[...] = total[mine, :] + other[...]
    out_less[...] = landed


def body(
    regions,
    transitions,
    tile_cols,
    tile_count,
    publish,
    reward,
    value_init,
    anchor,
    goal_segment_index,
    routes,
):
    blocks, kmax, tile, _ = transitions.shape
    width = anchor.shape[1]
    tiles, cols, pairs = dims(blocks, kmax)
    columns = plan(tile_cols, tile_count)
    vmem = pl.BlockSpec(memory_space=pltpu.VMEM)
    hbm = pl.BlockSpec(memory_space=pltpu.HBM)
    out, less = pl.pallas_call(
        functools.partial(kernel, (blocks, kmax, regions)),
        out_shape=[jax.ShapeDtypeStruct((blocks // 2, tile), F32)] * 2,
        in_specs=[vmem, vmem, vmem, vmem, vmem, hbm, hbm, hbm],
        out_specs=[vmem, vmem],
        scratch_shapes=[
            pltpu.VMEM((tiles, tile, tile), BF16),
            pltpu.VMEM((blocks * tile, width), BF16),
            pltpu.VMEM((blocks * tile, width), BF16),
            pltpu.VMEM((blocks, width, tile), F32),
            pltpu.VMEM((cols + 1, width, tile), BF16),
            pltpu.VMEM((cols + 1, width, tile), BF16),
            pltpu.VMEM((4, width, tile), BF16),
            pltpu.VMEM((4, width, tile), BF16),
            pltpu.VMEM((4, blocks * tile, tile), BF16),
            pltpu.VMEM((routes.shape[1], routes.shape[0]), jnp.int32),
            pltpu.VMEM((width, tile), jnp.int32),
            pltpu.VMEM((blocks, width, tile), F32),
            pltpu.VMEM((blocks + 1, width, tile), BF16),
            pltpu.VMEM((pairs + 1, width, tile), F32),
            pltpu.VMEM((4, width, tile), BF16),
            pltpu.VMEM((4, width, tile), BF16),
            pltpu.VMEM((blocks, tile), F32),
            pltpu.VMEM((blocks // 2, tile), F32),
            pltpu.VMEM((4, 8, tile), F32),
            pltpu.VMEM((2, 4, 8, tile), F32),
            pltpu.VMEM((8, 128), jnp.int32),
            pltpu.SMEM((8, 128), jnp.int32),
            pltpu.SemaphoreType.DMA((4,)),
            pltpu.SemaphoreType.DMA((3, 4)),
            pltpu.SemaphoreType.DMA((3, 4)),
            pltpu.SemaphoreType.DMA((2,)),
            pltpu.SemaphoreType.DMA((2, 4)),
            pltpu.SemaphoreType.DMA((2, 4)),
        ],
        compiler_params=pltpu.CompilerParams(
            collective_id=0, has_side_effects=True, vmem_limit_bytes=56 * 1024 * 1024
        ),
    )(
        columns,
        publish[0],
        reward.reshape(blocks, tile),
        goal_segment_index.reshape(1, width),
        routes.T,
        transitions.reshape(tiles, tile, tile),
        value_init,
        anchor,
    )
    return (out - less).reshape(-1)


def solution(mesh):
    return jax.shard_map(
        functools.partial(body, mesh.shape["region"]),
        mesh=mesh,
        in_specs=(
            P(("metro", "region"), None, None, None),
            P(("metro", "region"), None),
            P(("metro", "region")),
            P(("metro", "region"), None, None),
            P(("metro", "region")),
            P(("metro", "region"), "dest"),
            P(("metro", "region"), "dest"),
            P(("metro", "dest")),
            P(("metro", "dest"), None),
        ),
        out_specs=P(("metro", "region", "dest")),
        check_vma=False,
    )
```

```python
import functools

import jax
import jax.numpy as jnp
from jax import lax
from jax.experimental import pallas as pl
from jax.experimental.pallas import tpu as pltpu
from jax.sharding import PartitionSpec as P

OFFSETS = (-2, -1, 1, 2)
ORDER = (1, 2, 0, 3)
MESH = pl.DeviceIdType.MESH
F32 = jnp.float32
BF16 = jnp.bfloat16
LAST = (((1,), (1,)), ((), ()))


def dims(blocks, kmax):
    tiles = blocks * kmax
    cols = blocks + 4
    pairs = (tiles + cols) // 2
    return tiles, cols, pairs


def plan(tile_cols, tile_count):
    blocks, kmax = tile_cols.shape
    tiles, cols, _ = dims(blocks, kmax)
    live = lax.broadcasted_iota(jnp.int32, (blocks, kmax), 1) < tile_count[:, None]
    col = jnp.where(live, tile_cols, cols).reshape(1, tiles)
    return jnp.pad(col, ((0, 0), (0, 128 - tiles)), constant_values=cols)


def make_lists(col, row, lane, shape):
    blocks, kmax = shape
    tiles, cols, pairs = dims(blocks, kmax)

    def down(x):
        return jnp.sum(x, axis=0, keepdims=True)

    def across(x):
        return jnp.sum(x, axis=1, keepdims=True)

    col = jnp.where(lane[:1] < tiles, col, cols)
    def order(c):
        return jnp.where(c >= blocks, c - blocks, c + 4)

    by_lane = jnp.broadcast_to(col, row.shape)
    by_row = by_lane.T
    rank = down(jnp.where((by_lane == by_row) & (row < lane), 1, 0))
    count_row = down(jnp.where((by_row == lane) & (lane < cols), 1, 0))
    count_col = across(jnp.where((by_lane == row) & (row < cols), 1, 0))
    padded_row = jnp.bitwise_and(count_row + 1, -2)
    padded_col = jnp.bitwise_and(count_col + 1, -2)
    start_row = down(jnp.where(order(row) < order(lane), padded_col, 0))
    start_col = across(jnp.where(order(lane) < order(row), padded_row, 0))
    first = down(jnp.where(order(row) < order(by_lane), padded_col, 0))
    spot = jnp.where(col < cols, first + rank, -1)
    hit = jnp.broadcast_to(spot, row.shape).T == lane
    tile_at = down(jnp.where(hit, row, 0))
    owner = lax.shift_right_logical(row * (256 // kmax + 1), 8)
    block_at = blocks + down(jnp.where(hit, owner - blocks, 0))
    keep = 1 - down(jnp.where((start_col == 2 * lane) & (count_col > 0), 1, 0))
    last = jnp.where(count_row > 0, lax.shift_right_logical(start_row + padded_row, 1) - 1, pairs)
    return jnp.concatenate([col, tile_at, block_at, keep, last, col, col, col], 0)


def kernel(
    shape,
    columns,
    publish,
    reward,
    goal,
    routes,
    trans_hbm,
    init_hbm,
    anchor_hbm,
    out,
    trans,
    init,
    anchor_in,
    anchor,
    ext1,
    ext2,
    piece1,
    piece2,
    hot,
    ids,
    gap,
    inv,
    flow_u,
    sums,
    part1,
    arr1,
    total,
    other,
    terms,
    away,
    table,
    lists,
    load_sem,
    send_sem,
    recv_sem,
    dest_sem,
    terms_send,
    terms_recv,
):
    blocks, kmax, regions = shape
    tiles, cols, pairs = dims(blocks, kmax)
    tile = 128
    me = lax.axis_index("region")
    side = lax.axis_index("dest")
    first_seg = me * (blocks * tile)
    of_col, of_tile, of_block, of_keep, of_last = range(5)

    load_init = pltpu.make_async_copy(init_hbm, init, load_sem.at[0])
    load_trans = pltpu.make_async_copy(trans_hbm, trans, load_sem.at[1])
    load_anchor = pltpu.make_async_copy(anchor_hbm, anchor_in, load_sem.at[2])
    load_init.start()
    load_trans.start()
    load_anchor.start()

    def inside(by):
        return (me + by >= 0) & (me + by < regions)

    barrier = pltpu.get_barrier_semaphore()
    pl.semaphore_signal(barrier, inc=1, device_id={"dest": 1 - side}, device_id_type=MESH)
    for by in OFFSETS:
        @pl.when(inside(by))
        def _():
            for d in range(2):
                pl.semaphore_signal(barrier, inc=1, device_id={"region": me + by, "dest": d}, device_id_type=MESH)

    zero = jnp.zeros((tile, tile), BF16)
    ext1[cols] = zero
    ext2[cols] = zero
    flow_u[blocks] = zero
    sums[pairs] = jnp.zeros((tile, tile), F32)
    for j, by in enumerate(OFFSETS):
        @pl.when(jnp.logical_not(inside(by)))
        def _():
            ext1[blocks + j] = zero
            ext2[blocks + j] = zero

        @pl.when(jnp.logical_not(inside(-by)))
        def _():
            arr1[j] = zero
            for d in range(2):
                away[d, j] = jnp.zeros((8, tile), F32)

    row = lax.broadcasted_iota(jnp.int32, (tile, tile), 0)
    lane = lax.broadcasted_iota(jnp.int32, (tile, tile), 1)

    def make_hot(c, carry):
        for j in range(4):
            pub = publish[j : j + 1, :]
            hit = (row + c * tile) == pub
            hot[j, pl.ds(pl.multiple_of(c * tile, tile), tile), :] = jnp.where(hit, 1.0, 0.0).astype(BF16)
        return carry

    lax.fori_loop(0, blocks, make_hot, 0, unroll=True)

    load_init.wait()

    def make_start(b, carry):
        block = init[pl.ds(pl.multiple_of(b * tile, tile), tile), :].astype(F32)
        ext1[b] = jnp.exp(block.T).astype(BF16)
        return carry

    lax.fori_loop(0, blocks, make_start, 0, unroll=True)

    def exchange(phase, source, target, base, sign):
        def copy(j):
            return pltpu.make_async_remote_copy(
                src_ref=source.at[j],
                dst_ref=target.at[base + j],
                send_sem=send_sem.at[phase, j],
                recv_sem=recv_sem.at[phase, j],
                device_id={"region": me + sign * OFFSETS[j]},
                device_id_type=MESH,
            )

        def start(j):
            @pl.when(inside(sign * OFFSETS[j]))
            def _():
                copy(j).start()

        def wait():
            for j in range(4):
                @pl.when(inside(-sign * OFFSETS[j]))
                def _():
                    copy(j).wait_recv()

        def finish():
            for j in range(4):
                @pl.when(inside(sign * OFFSETS[j]))
                def _():
                    copy(j).wait_send()

        return start, wait, finish

    def publish_rows(ext, piece, start):
        whole = jnp.concatenate([ext[b] for b in range(blocks)], 1)
        for j in ORDER:
            picked = jnp.dot(whole, hot[j], preferred_element_type=F32)
            piece[j] = picked.astype(BF16)
            start(j)

    def product(ext, b):
        left = jnp.concatenate([ext[lists[of_col, b * kmax + k]] for k in range(kmax)], 1)
        right = jnp.concatenate([trans[b * kmax + k] for k in range(kmax)], 1)
        return lax.dot_general(left, right, LAST, preferred_element_type=F32)

    def bonus(b):
        return jnp.where(gap[...] == b * tile, 1.0, 0.0)

    neighbours = 1
    for by in OFFSETS:
        neighbours = neighbours + 2 * inside(by).astype(jnp.int32)
    pl.semaphore_wait(barrier, neighbours)

    start1, wait1, finish1 = exchange(0, piece1, ext1, blocks, -1)
    start2, wait2, finish2 = exchange(1, piece2, ext2, blocks, -1)
    start3, wait3, finish3 = exchange(2, part1, arr1, 0, 1)

    publish_rows(ext1, piece1, start1)

    gap[...] = jnp.broadcast_to(goal[...] - first_seg, (tile, tile)).T - lane
    ids[...] = routes[...] - first_seg
    group = 4

    def count(q, acc):
        highs, lows = [], []
        for g in range(group):
            line = ids[pl.ds(q * group + g, 1), :]
            low = jnp.bitwise_and(line, tile - 1)
            high = lax.shift_right_arithmetic(line, 7)
            lows.append(jnp.where(row == low, 1.0, 0.0).astype(BF16))
            highs.append(jnp.where(row[:blocks] == high, 1.0, 0.0).astype(BF16))
        return acc + lax.dot_general(
            jnp.concatenate(highs, 1), jnp.concatenate(lows, 1), LAST, preferred_element_type=F32
        )

    table[...] = make_lists(columns[...], row, lane, (blocks, kmax))
    load_lists = pltpu.make_async_copy(table, lists, load_sem.at[3])
    load_lists.start()
    groups = ids.shape[0] // group
    counted = lax.fori_loop(0, groups // 2, count, jnp.zeros((blocks, tile), F32), unroll=True)
    load_lists.wait()
    load_trans.wait()
    wait1()

    def first_backup(b, carry):
        y = product(ext1, b) + bonus(b)
        ext2[b] = (jnp.exp(reward[pl.ds(b, 1), :]) * y).astype(BF16)
        return carry

    lax.fori_loop(0, blocks, first_backup, 0, unroll=True)
    publish_rows(ext2, piece2, start2)

    load_anchor.wait()

    total[...] = lax.fori_loop(groups // 2, groups, count, counted, unroll=True)

    def turn(b, carry):
        block = anchor_in[pl.ds(pl.multiple_of(b * tile, tile), tile), :].astype(F32).T
        anchor[b] = block
        here = pl.ds(b, 1)
        total[here, :] = total[here, :] - 2.0 * jnp.sum(block, axis=0, keepdims=True)
        return carry

    lax.fori_loop(0, blocks, turn, 0, unroll=True)
    wait2()

    def second_backup(b, carry):
        y = product(ext2, b) + bonus(b)
        w = 1.0 / y
        inv[b] = w
        flow_u[b] = (anchor[b] * w).astype(BF16)
        return carry

    lax.fori_loop(0, blocks, second_backup, 0, unroll=True)

    early = min(((kmax - 1) * blocks + 4) // 2, pairs)

    def spread(low, high, acc):
        def step(t, acc):
            left = jnp.concatenate(
                [flow_u[lists[of_block, 2 * t + h]] for h in range(2)], 1
            )
            right = jnp.concatenate([trans[lists[of_tile, 2 * t + h]] for h in range(2)], 0)
            new = jnp.dot(left, right, preferred_element_type=F32)
            acc = acc * lists[of_keep, t].astype(F32) + new
            sums[t] = acc
            return acc

        return lax.fori_loop(low, high, step, acc, unroll=True)

    def arrive(arr, c):
        left = jnp.concatenate([arr[j] for j in range(4)], 1)
        rows = pl.ds(pl.multiple_of(c * tile, tile), tile)
        right = jnp.concatenate([hot[j, rows, :] for j in range(4)], 1)
        back = lax.dot_general(left, right, LAST, preferred_element_type=F32)
        return anchor[c] + ext2[c].astype(F32) * back

    none = jnp.zeros((tile, tile), F32)
    acc = spread(0, early, none)
    for j in ORDER:
        part1[j] = sums[lists[of_last, blocks + j]].astype(BF16)
        start3(j)
    spread(early, pairs, acc)

    def local_flow(c, carry):
        anchor[c] = anchor[c] + ext2[c].astype(F32) * sums[lists[of_last, c]]
        return carry

    lax.fori_loop(0, blocks, local_flow, 0, unroll=True)
    wait3()

    def first_flow(c, carry):
        flow = arrive(arr1, c)
        flow_u[c] = (flow * inv[c]).astype(BF16)
        here = pl.ds(c, 1)
        total[here, :] = total[here, :] - jnp.sum(flow, axis=0, keepdims=True)
        return carry

    lax.fori_loop(0, blocks, first_flow, 0, unroll=True)
    acc = spread(0, early, none)

    def term_copy(j, d, slot):
        return pltpu.make_async_remote_copy(
            src_ref=terms.at[j],
            dst_ref=away.at[slot, j],
            send_sem=terms_send.at[d, j],
            recv_sem=terms_recv.at[slot, j],
            device_id={"region": me + OFFSETS[j], "dest": d},
            device_id_type=MESH,
        )

    for j in ORDER:
        flow = sums[lists[of_last, blocks + j]] * ext2[blocks + j].astype(F32)
        terms[j] = jnp.sum(flow.reshape(tile // 8, 8, tile), axis=0)

        @pl.when(inside(OFFSETS[j]))
        def _():
            for d in range(2):
                term_copy(j, d, side).start()

    spread(early, pairs, acc)

    def second_flow(c, carry):
        flow = ext2[c].astype(F32) * sums[lists[of_last, c]]
        here = pl.ds(c, 1)
        total[here, :] = total[here, :] - jnp.sum(flow, axis=0, keepdims=True)
        return carry

    lax.fori_loop(0, blocks, second_flow, 0, unroll=True)

    share = blocks // 2
    mine = pl.ds(pl.multiple_of(side * share, share), share)
    theirs = pl.ds(pl.multiple_of((1 - side) * share, share), share)
    swap = pltpu.make_async_remote_copy(
        src_ref=total.at[theirs],
        dst_ref=other,
        send_sem=dest_sem.at[0],
        recv_sem=dest_sem.at[1],
        device_id={"dest": 1 - side},
        device_id_type=MESH,
    )
    swap.start()
    finish1()
    finish2()
    finish3()
    for j in range(4):
        @pl.when(inside(OFFSETS[j]))
        def _():
            for d in range(2):
                term_copy(j, d, side).wait_send()

        @pl.when(inside(-OFFSETS[j]))
        def _():
            for d in range(2):
                term_copy(j, d, d).wait_recv()

    whole = jnp.concatenate([away[0, j] + away[1, j] for j in range(4)], 1)
    high = whole.astype(BF16)
    rest = whole - high.astype(F32)
    middle = rest.astype(BF16)
    low = (rest - middle.astype(F32)).astype(BF16)
    left = jnp.concatenate([high, middle, low, jnp.zeros_like(low)], 0)
    lines = []
    for i in range(share):
        rows = pl.ds(pl.multiple_of((side * share + i) * tile, tile), tile)
        right = jnp.concatenate([hot[j, rows, :] for j in range(4)], 1)
        back = lax.dot_general(left, right, LAST, preferred_element_type=F32)
        lines.append(jnp.sum(back, axis=0, keepdims=True))
    landed = jnp.concatenate(lines, 0)
    swap.wait()
    out[...] = total[mine, :] + other[...] - landed


def body(
    regions,
    transitions,
    tile_cols,
    tile_count,
    publish,
    reward,
    value_init,
    anchor,
    goal_segment_index,
    routes,
):
    blocks, kmax, tile, _ = transitions.shape
    width = anchor.shape[1]
    tiles, cols, pairs = dims(blocks, kmax)
    columns = plan(tile_cols, tile_count)
    vmem = pl.BlockSpec(memory_space=pltpu.VMEM)
    hbm = pl.BlockSpec(memory_space=pltpu.HBM)
    out = pl.pallas_call(
        functools.partial(kernel, (blocks, kmax, regions)),
        out_shape=jax.ShapeDtypeStruct((blocks // 2, tile), F32),
        in_specs=[vmem, vmem, vmem, vmem, vmem, hbm, hbm, hbm],
        out_specs=vmem,
        scratch_shapes=[
            pltpu.VMEM((tiles, tile, tile), BF16),
            pltpu.VMEM((blocks * tile, width), BF16),
            pltpu.VMEM((blocks * tile, width), BF16),
            pltpu.VMEM((blocks, width, tile), F32),
            pltpu.VMEM((cols + 1, width, tile), BF16),
            pltpu.VMEM((cols + 1, width, tile), BF16),
            pltpu.VMEM((4, width, tile), BF16),
            pltpu.VMEM((4, width, tile), BF16),
            pltpu.VMEM((4, blocks * tile, tile), BF16),
            pltpu.VMEM((routes.shape[1], routes.shape[0]), jnp.int32),
            pltpu.VMEM((width, tile), jnp.int32),
            pltpu.VMEM((blocks, width, tile), F32),
            pltpu.VMEM((blocks + 1, width, tile), BF16),
            pltpu.VMEM((pairs + 1, width, tile), F32),
            pltpu.VMEM((4, width, tile), BF16),
            pltpu.VMEM((4, width, tile), BF16),
            pltpu.VMEM((blocks, tile), F32),
            pltpu.VMEM((blocks // 2, tile), F32),
            pltpu.VMEM((4, 8, tile), F32),
            pltpu.VMEM((2, 4, 8, tile), F32),
            pltpu.VMEM((8, 128), jnp.int32),
            pltpu.SMEM((8, 128), jnp.int32),
            pltpu.SemaphoreType.DMA((4,)),
            pltpu.SemaphoreType.DMA((3, 4)),
            pltpu.SemaphoreType.DMA((3, 4)),
            pltpu.SemaphoreType.DMA((2,)),
            pltpu.SemaphoreType.DMA((2, 4)),
            pltpu.SemaphoreType.DMA((2, 4)),
        ],
        compiler_params=pltpu.CompilerParams(
            collective_id=0, has_side_effects=True, vmem_limit_bytes=56 * 1024 * 1024
        ),
    )(
        columns,
        publish[0],
        reward.reshape(blocks, tile),
        goal_segment_index.reshape(1, width),
        routes.T,
        transitions.reshape(tiles, tile, tile),
        value_init,
        anchor,
    )
    return out.reshape(-1)


def solution(mesh):
    return jax.shard_map(
        functools.partial(body, mesh.shape["region"]),
        mesh=mesh,
        in_specs=(
            P(("metro", "region"), None, None, None),
            P(("metro", "region"), None),
            P(("metro", "region")),
            P(("metro", "region"), None, None),
            P(("metro", "region")),
            P(("metro", "region"), "dest"),
            P(("metro", "region"), "dest"),
            P(("metro", "dest")),
            P(("metro", "dest"), None),
        ),
        out_specs=P(("metro", "region", "dest")),
        check_vma=False,
    )
```

```python
import functools

import jax
import jax.numpy as jnp
from jax import lax
from jax.experimental import pallas as pl
from jax.experimental.pallas import tpu as pltpu
from jax.sharding import PartitionSpec as P

OFFSETS = (-2, -1, 1, 2)
ORDER = (1, 2, 0, 3)
MESH = pl.DeviceIdType.MESH
F32 = jnp.float32
BF16 = jnp.bfloat16
LAST = (((1,), (1,)), ((), ()))


def dims(blocks, kmax):
    tiles = blocks * kmax
    cols = blocks + 4
    pairs = (tiles + cols) // 2
    return tiles, cols, pairs


def make_lists(tile_cols, tile_count, row, lane, shape):
    blocks, kmax = shape
    tiles, cols, pairs = dims(blocks, kmax)

    def down(x):
        return jnp.sum(x, axis=0, keepdims=True)

    def across(x):
        return jnp.sum(x, axis=1, keepdims=True)

    def grid(width, dim):
        return lax.broadcasted_iota(jnp.int32, (row.shape[0], width), dim)

    def owner_of(p):
        return lax.shift_right_logical(p * (256 // kmax + 1), 8)

    place = owner_of(grid(kmax, 0))
    turn = grid(kmax, 0) - place * kmax
    cells = jnp.zeros(place.shape, jnp.int32)
    for b in range(blocks):
        cells = jnp.where(place == b, tile_cols[b : b + 1, :], cells)
    cell = across(jnp.where(grid(kmax, 1) == turn, cells, 0))
    alive = across(jnp.where(grid(blocks, 1) == owner_of(grid(blocks, 0)), tile_count, 0))
    by_row = jnp.broadcast_to(jnp.where(turn[:, :1] < alive, cell, cols), row.shape)
    by_lane = by_row.T
    col = by_lane[:1]
    def order(c):
        return jnp.where(c >= blocks, c - blocks, c + 4)

    rank = down(jnp.where((by_lane == by_row) & (row < lane), 1, 0))
    count_row = down(jnp.where((by_row == lane) & (lane < cols), 1, 0))
    count_col = across(jnp.where((by_lane == row) & (row < cols), 1, 0))
    padded_row = jnp.bitwise_and(count_row + 1, -2)
    padded_col = jnp.bitwise_and(count_col + 1, -2)
    start_row = down(jnp.where(order(row) < order(lane), padded_col, 0))
    start_col = across(jnp.where(order(lane) < order(row), padded_row, 0))
    first = down(jnp.where(order(row) < order(by_lane), padded_col, 0))
    spot = jnp.where(col < cols, first + rank, -1)
    hit = jnp.broadcast_to(spot, row.shape).T == lane
    tile_at = down(jnp.where(hit, row, 0))
    owner = owner_of(row)
    block_at = blocks + down(jnp.where(hit, owner - blocks, 0))
    keep = 1 - down(jnp.where((start_col == 2 * lane) & (count_col > 0), 1, 0))
    last = jnp.where(count_row > 0, lax.shift_right_logical(start_row + padded_row, 1) - 1, pairs)
    return jnp.concatenate([col, tile_at, block_at, keep, last, col, col, col], 0)


def kernel(
    shape,
    tile_cols,
    tile_count,
    publish,
    reward,
    goal,
    routes,
    trans_hbm,
    init_hbm,
    anchor_hbm,
    out,
    trans,
    init,
    anchor_in,
    anchor,
    ext1,
    ext2,
    piece1,
    piece2,
    hot,
    ids,
    gap,
    inv,
    flow_u,
    sums,
    part1,
    arr1,
    total,
    other,
    terms,
    away,
    table,
    lists,
    load_sem,
    send_sem,
    recv_sem,
    dest_sem,
    terms_send,
    terms_recv,
):
    blocks, kmax, regions = shape
    tiles, cols, pairs = dims(blocks, kmax)
    tile = 128
    me = lax.axis_index("region")
    side = lax.axis_index("dest")
    first_seg = me * (blocks * tile)
    of_col, of_tile, of_block, of_keep, of_last = range(5)

    load_init = pltpu.make_async_copy(init_hbm, init, load_sem.at[0])
    load_trans = pltpu.make_async_copy(trans_hbm, trans, load_sem.at[1])
    load_anchor = pltpu.make_async_copy(anchor_hbm, anchor_in, load_sem.at[2])
    load_init.start()
    load_trans.start()
    load_anchor.start()

    def inside(by):
        return (me + by >= 0) & (me + by < regions)

    barrier = pltpu.get_barrier_semaphore()
    pl.semaphore_signal(barrier, inc=1, device_id={"dest": 1 - side}, device_id_type=MESH)
    for by in OFFSETS:
        @pl.when(inside(by))
        def _():
            for d in range(2):
                pl.semaphore_signal(barrier, inc=1, device_id={"region": me + by, "dest": d}, device_id_type=MESH)

    zero = jnp.zeros((tile, tile), BF16)
    ext1[cols] = zero
    ext2[cols] = zero
    flow_u[blocks] = zero
    sums[pairs] = jnp.zeros((tile, tile), F32)
    for j, by in enumerate(OFFSETS):
        @pl.when(jnp.logical_not(inside(by)))
        def _():
            ext1[blocks + j] = zero
            ext2[blocks + j] = zero

        @pl.when(jnp.logical_not(inside(-by)))
        def _():
            arr1[j] = zero
            for d in range(2):
                away[d, j] = jnp.zeros((8, tile), F32)

    row = lax.broadcasted_iota(jnp.int32, (tile, tile), 0)
    lane = lax.broadcasted_iota(jnp.int32, (tile, tile), 1)

    def make_hot(c, carry):
        for j in range(4):
            pub = publish[j : j + 1, :]
            hit = (row + c * tile) == pub
            hot[j, pl.ds(pl.multiple_of(c * tile, tile), tile), :] = jnp.where(hit, 1.0, 0.0).astype(BF16)
        return carry

    lax.fori_loop(0, blocks, make_hot, 0, unroll=True)

    load_init.wait()

    def make_start(b, carry):
        block = init[pl.ds(pl.multiple_of(b * tile, tile), tile), :].astype(F32)
        ext1[b] = jnp.exp(block.T).astype(BF16)
        return carry

    lax.fori_loop(0, blocks, make_start, 0, unroll=True)

    def exchange(phase, source, target, base, sign):
        def copy(j):
            return pltpu.make_async_remote_copy(
                src_ref=source.at[j],
                dst_ref=target.at[base + j],
                send_sem=send_sem.at[phase, j],
                recv_sem=recv_sem.at[phase, j],
                device_id={"region": me + sign * OFFSETS[j]},
                device_id_type=MESH,
            )

        def start(j):
            @pl.when(inside(sign * OFFSETS[j]))
            def _():
                copy(j).start()

        def wait():
            for j in range(4):
                @pl.when(inside(-sign * OFFSETS[j]))
                def _():
                    copy(j).wait_recv()

        def finish():
            for j in range(4):
                @pl.when(inside(sign * OFFSETS[j]))
                def _():
                    copy(j).wait_send()

        return start, wait, finish

    def publish_rows(ext, piece, start):
        whole = jnp.concatenate([ext[b] for b in range(blocks)], 1)
        for j in ORDER:
            picked = jnp.dot(whole, hot[j], preferred_element_type=F32)
            piece[j] = picked.astype(BF16)
            start(j)

    def product(ext, b):
        left = jnp.concatenate([ext[lists[of_col, b * kmax + k]] for k in range(kmax)], 1)
        right = jnp.concatenate([trans[b * kmax + k] for k in range(kmax)], 1)
        return lax.dot_general(left, right, LAST, preferred_element_type=F32)

    def bonus(b):
        return jnp.where(gap[...] == b * tile, 1.0, 0.0)

    neighbours = 1
    for by in OFFSETS:
        neighbours = neighbours + 2 * inside(by).astype(jnp.int32)
    pl.semaphore_wait(barrier, neighbours)

    start1, wait1, finish1 = exchange(0, piece1, ext1, blocks, -1)
    start2, wait2, finish2 = exchange(1, piece2, ext2, blocks, -1)
    start3, wait3, finish3 = exchange(2, part1, arr1, 0, 1)

    publish_rows(ext1, piece1, start1)

    gap[...] = jnp.broadcast_to(goal[...] - first_seg, (tile, tile)).T - lane
    ids[...] = routes[...] - first_seg
    group = 4

    def count(q, acc):
        highs, lows = [], []
        for g in range(group):
            line = ids[pl.ds(q * group + g, 1), :]
            low = jnp.bitwise_and(line, tile - 1)
            high = lax.shift_right_arithmetic(line, 7)
            lows.append(jnp.where(row == low, 1.0, 0.0).astype(BF16))
            highs.append(jnp.where(row[:blocks] == high, 1.0, 0.0).astype(BF16))
        return acc + lax.dot_general(
            jnp.concatenate(highs, 1), jnp.concatenate(lows, 1), LAST, preferred_element_type=F32
        )

    table[...] = make_lists(tile_cols[...], tile_count[...], row, lane, (blocks, kmax))
    load_lists = pltpu.make_async_copy(table, lists, load_sem.at[3])
    load_lists.start()
    groups = ids.shape[0] // group
    counted = lax.fori_loop(0, groups // 2, count, jnp.zeros((blocks, tile), F32), unroll=True)
    load_lists.wait()
    load_trans.wait()
    wait1()

    def first_backup(b, carry):
        y = product(ext1, b) + bonus(b)
        ext2[b] = (jnp.exp(reward[pl.ds(b, 1), :]) * y).astype(BF16)
        return carry

    lax.fori_loop(0, blocks, first_backup, 0, unroll=True)
    publish_rows(ext2, piece2, start2)

    load_anchor.wait()

    total[...] = lax.fori_loop(groups // 2, groups, count, counted, unroll=True)

    def turn(b, carry):
        block = anchor_in[pl.ds(pl.multiple_of(b * tile, tile), tile), :].astype(F32).T
        anchor[b] = block
        here = pl.ds(b, 1)
        total[here, :] = total[here, :] - 2.0 * jnp.sum(block, axis=0, keepdims=True)
        return carry

    lax.fori_loop(0, blocks, turn, 0, unroll=True)
    wait2()

    def second_backup(b, carry):
        y = product(ext2, b) + bonus(b)
        w = 1.0 / y
        inv[b] = w
        flow_u[b] = (anchor[b] * w).astype(BF16)
        return carry

    lax.fori_loop(0, blocks, second_backup, 0, unroll=True)

    early = min(((kmax - 1) * blocks + 4) // 2, pairs)

    def spread(low, high, acc):
        def step(t, acc):
            left = jnp.concatenate(
                [flow_u[lists[of_block, 2 * t + h]] for h in range(2)], 1
            )
            right = jnp.concatenate([trans[lists[of_tile, 2 * t + h]] for h in range(2)], 0)
            new = jnp.dot(left, right, preferred_element_type=F32)
            acc = acc * lists[of_keep, t].astype(F32) + new
            sums[t] = acc
            return acc

        return lax.fori_loop(low, high, step, acc, unroll=True)

    def arrive(arr, c):
        left = jnp.concatenate([arr[j] for j in range(4)], 1)
        rows = pl.ds(pl.multiple_of(c * tile, tile), tile)
        right = jnp.concatenate([hot[j, rows, :] for j in range(4)], 1)
        back = lax.dot_general(left, right, LAST, preferred_element_type=F32)
        return anchor[c] + ext2[c].astype(F32) * back

    none = jnp.zeros((tile, tile), F32)
    acc = spread(0, early, none)
    for j in ORDER:
        part1[j] = sums[lists[of_last, blocks + j]].astype(BF16)
        start3(j)
    spread(early, pairs, acc)

    def local_flow(c, carry):
        anchor[c] = anchor[c] + ext2[c].astype(F32) * sums[lists[of_last, c]]
        return carry

    lax.fori_loop(0, blocks, local_flow, 0, unroll=True)
    wait3()

    def first_flow(c, carry):
        flow = arrive(arr1, c)
        flow_u[c] = (flow * inv[c]).astype(BF16)
        here = pl.ds(c, 1)
        total[here, :] = total[here, :] - jnp.sum(flow, axis=0, keepdims=True)
        return carry

    lax.fori_loop(0, blocks, first_flow, 0, unroll=True)
    acc = spread(0, early, none)

    def term_copy(j, d, slot):
        return pltpu.make_async_remote_copy(
            src_ref=terms.at[j],
            dst_ref=away.at[slot, j],
            send_sem=terms_send.at[d, j],
            recv_sem=terms_recv.at[slot, j],
            device_id={"region": me + OFFSETS[j], "dest": d},
            device_id_type=MESH,
        )

    for j in ORDER:
        flow = sums[lists[of_last, blocks + j]] * ext2[blocks + j].astype(F32)
        terms[j] = jnp.sum(flow.reshape(tile // 8, 8, tile), axis=0)

        @pl.when(inside(OFFSETS[j]))
        def _():
            for d in range(2):
                term_copy(j, d, side).start()

    spread(early, pairs, acc)

    def second_flow(c, carry):
        flow = ext2[c].astype(F32) * sums[lists[of_last, c]]
        here = pl.ds(c, 1)
        total[here, :] = total[here, :] - jnp.sum(flow, axis=0, keepdims=True)
        return carry

    lax.fori_loop(0, blocks, second_flow, 0, unroll=True)

    share = blocks // 2
    mine = pl.ds(pl.multiple_of(side * share, share), share)
    theirs = pl.ds(pl.multiple_of((1 - side) * share, share), share)
    swap = pltpu.make_async_remote_copy(
        src_ref=total.at[theirs],
        dst_ref=other,
        send_sem=dest_sem.at[0],
        recv_sem=dest_sem.at[1],
        device_id={"dest": 1 - side},
        device_id_type=MESH,
    )
    swap.start()
    finish1()
    finish2()
    finish3()
    for j in range(4):
        @pl.when(inside(OFFSETS[j]))
        def _():
            for d in range(2):
                term_copy(j, d, side).wait_send()

        @pl.when(inside(-OFFSETS[j]))
        def _():
            for d in range(2):
                term_copy(j, d, d).wait_recv()

    whole = jnp.concatenate([away[0, j] + away[1, j] for j in range(4)], 1)
    high = whole.astype(BF16)
    rest = whole - high.astype(F32)
    middle = rest.astype(BF16)
    low = (rest - middle.astype(F32)).astype(BF16)
    left = jnp.concatenate([high, middle, low, jnp.zeros_like(low)], 0)
    lines = []
    for i in range(share):
        rows = pl.ds(pl.multiple_of((side * share + i) * tile, tile), tile)
        right = jnp.concatenate([hot[j, rows, :] for j in range(4)], 1)
        back = lax.dot_general(left, right, LAST, preferred_element_type=F32)
        lines.append(jnp.sum(back, axis=0, keepdims=True))
    landed = jnp.concatenate(lines, 0)
    swap.wait()
    out[...] = total[mine, :] + other[...] - landed


def body(
    regions,
    transitions,
    tile_cols,
    tile_count,
    publish,
    reward,
    value_init,
    anchor,
    goal_segment_index,
    routes,
):
    blocks, kmax, tile, _ = transitions.shape
    width = anchor.shape[1]
    tiles, cols, pairs = dims(blocks, kmax)
    vmem = pl.BlockSpec(memory_space=pltpu.VMEM)
    hbm = pl.BlockSpec(memory_space=pltpu.HBM)
    out = pl.pallas_call(
        functools.partial(kernel, (blocks, kmax, regions)),
        out_shape=jax.ShapeDtypeStruct((blocks // 2, tile), F32),
        in_specs=[vmem, vmem, vmem, vmem, vmem, vmem, hbm, hbm, hbm],
        out_specs=vmem,
        scratch_shapes=[
            pltpu.VMEM((tiles, tile, tile), BF16),
            pltpu.VMEM((blocks * tile, width), BF16),
            pltpu.VMEM((blocks * tile, width), BF16),
            pltpu.VMEM((blocks, width, tile), F32),
            pltpu.VMEM((cols + 1, width, tile), BF16),
            pltpu.VMEM((cols + 1, width, tile), BF16),
            pltpu.VMEM((4, width, tile), BF16),
            pltpu.VMEM((4, width, tile), BF16),
            pltpu.VMEM((4, blocks * tile, tile), BF16),
            pltpu.VMEM((routes.shape[1], routes.shape[0]), jnp.int32),
            pltpu.VMEM((width, tile), jnp.int32),
            pltpu.VMEM((blocks, width, tile), F32),
            pltpu.VMEM((blocks + 1, width, tile), BF16),
            pltpu.VMEM((pairs + 1, width, tile), F32),
            pltpu.VMEM((4, width, tile), BF16),
            pltpu.VMEM((4, width, tile), BF16),
            pltpu.VMEM((blocks, tile), F32),
            pltpu.VMEM((blocks // 2, tile), F32),
            pltpu.VMEM((4, 8, tile), F32),
            pltpu.VMEM((2, 4, 8, tile), F32),
            pltpu.VMEM((8, 128), jnp.int32),
            pltpu.SMEM((8, 128), jnp.int32),
            pltpu.SemaphoreType.DMA((4,)),
            pltpu.SemaphoreType.DMA((3, 4)),
            pltpu.SemaphoreType.DMA((3, 4)),
            pltpu.SemaphoreType.DMA((2,)),
            pltpu.SemaphoreType.DMA((2, 4)),
            pltpu.SemaphoreType.DMA((2, 4)),
        ],
        compiler_params=pltpu.CompilerParams(
            collective_id=0, has_side_effects=True, vmem_limit_bytes=56 * 1024 * 1024
        ),
    )(
        tile_cols,
        tile_count.reshape(1, blocks),
        publish[0],
        reward.reshape(blocks, tile),
        goal_segment_index.reshape(1, width),
        routes.T,
        transitions.reshape(tiles, tile, tile),
        value_init,
        anchor,
    )
    return out.reshape(-1)


def solution(mesh):
    return jax.shard_map(
        functools.partial(body, mesh.shape["region"]),
        mesh=mesh,
        in_specs=(
            P(("metro", "region"), None, None, None),
            P(("metro", "region"), None),
            P(("metro", "region")),
            P(("metro", "region"), None, None),
            P(("metro", "region")),
            P(("metro", "region"), "dest"),
            P(("metro", "region"), "dest"),
            P(("metro", "dest")),
            P(("metro", "dest"), None),
        ),
        out_specs=P(("metro", "region", "dest")),
        check_vma=False,
    )
```
